256 devices in a mesh: section: 4 (over z_lo, core), seq: 64 (over z_hi, x, y).
Axes of the slice: x: 4, y: 4, z: 8 (z_hi: 4, z_lo: 2; z = z_hi * 2 + z_lo), core: 2. Of those that a mesh axis runs over, the one named last changes fastest.
Arguments:
- queries: bfloat16 [4, 16384, 3072], P('section', 'seq'), may hold values from -0.75 to 0.75
- out_grads: bfloat16 [4, 16384, 3072], P('section', 'seq'), may hold values from -0.59765625 to 0.59765625
- logsumexp: float32 [4, 24, 16384], P('section', None, 'seq'), may hold values from 3.5 to 5.5
- shared_keys: bfloat16 [1024, 1024], P('seq'), may hold values from -48 to 48
- shared_values: bfloat16 [1024, 1024], P('seq'), may hold values from -6 to 6
- query_starts: int32 [64], P('seq'), may hold values from 0 to 16383, as said below
- slab_starts: int32 [64], P('seq'), may hold values from 0 to 16383, as said below
Outputs:
- query_grads: float32 [4, 16384, 3072], P('section', 'seq')
- key_grads: float32 [1024, 1024], P('seq', 'section')
- value_grads: float32 [1024, 1024], P('seq', 'section')
The draws below stay inside these ranges and needn't reach their ends.
Inputs may be any that keep to these rules, and one draw needn't show every extreme that they name: s * 256 <= query_starts[s] < (s + 1) * 256. j * 256 <= slab_starts[j] < (j + 1) * 256.
All inputs are finite; a program needn't handle non-finite values.
Results may differ from the reference program's by a relative error of at most 0.004.
Values may be sent and summed in bfloat16 or wider, within the bound.
No kernel may reach another device: no remote copies, remote signals or barrier semaphores. Data moves between devices by JAX's collectives and lax.ppermute only.
A program may use at most 128 MiB of HBM per device.

```python
import jax
import jax.numpy as jnp
from jax import lax

Q_HEADS = 24
KV_HEADS = 8
HEAD_DIM = 128
QDEV = 256
SLAB = 16
LAYERS = 4
SLABS = 64
QTOT = 16384
KTOT = 1024


def draw_query_starts(key, part):
    shard_base = jnp.arange(SLABS, dtype=jnp.int32) * QDEV
    jitter = jax.random.randint(jax.random.fold_in(key, 11), (SLABS,), 0, QDEV, dtype=jnp.int32)
    jitter = jitter.at[0].set(0).at[SLABS - 1].set(QDEV - 1)
    return shard_base + jitter


def draw_slab_starts(key, part):
    shard_base = jnp.arange(SLABS, dtype=jnp.int32) * QDEV
    jitter = jax.random.randint(jax.random.fold_in(key, 23), (SLABS,), 0, QDEV, dtype=jnp.int32)
    jitter = jitter.at[0].set(0).at[SLABS - 1].set(QDEV - 1)
    return shard_base + jitter


def levels(stream_key, extent, shards, smallest, top_value):
    def one(axis_at, parts):
        draws = jax.random.uniform(jax.random.fold_in(jax.random.fold_in(stream_key, 6), axis_at), (parts,), jnp.float32, smallest / len(shards), top_value / len(shards))
        return jnp.repeat(jnp.exp(draws), extent[axis_at] // parts).reshape((-1,) + (1,) * (len(extent) - axis_at - 1))

    level = one(*shards[0])
    for cut in shards[1:]:
        level = level * one(*cut)
    return level


def gaussian(stream_key, shape, width, reach, cuts=(), kind=jnp.bfloat16):
    level = levels(stream_key, shape, cuts, -0.22, 0.18) if cuts else 1.0
    drawn = jax.random.normal(stream_key, shape, jnp.float32) * width * level
    return jnp.minimum(jnp.maximum(drawn, -reach), reach).astype(kind)


def setup_inputs(seed: int = 0) -> dict:
    key_list = jax.random.split(jax.random.key(seed), 8)
    queries = gaussian(key_list[0], (LAYERS, QTOT, Q_HEADS * HEAD_DIM), 0.125, 0.75, ((0, 4), (1, 64)))
    out_grads = gaussian(key_list[1], (LAYERS, QTOT, Q_HEADS * HEAD_DIM), 0.1, 0.59765625, ((0, 4), (1, 64)))
    logsumexp = jnp.clip(3.5 + 2.0 * jax.random.uniform(key_list[2], (LAYERS, Q_HEADS, QTOT), jnp.float32) ** levels(key_list[2], (LAYERS, Q_HEADS, QTOT), ((0, 4), (2, 64)), -0.2, 0.2), 3.5, 5.5)
    shared_keys = gaussian(key_list[3], (KTOT, KV_HEADS * HEAD_DIM), 8.0, 48.0, ((0, 64),))
    shared_values = gaussian(key_list[4], (KTOT, KV_HEADS * HEAD_DIM), 1.0, 6.0, ((0, 64),))
    query_starts = draw_query_starts(jax.random.fold_in(key_list[7], 71), 0)
    slab_starts = draw_slab_starts(jax.random.fold_in(key_list[7], 71), 0)
    return dict(queries=queries, out_grads=out_grads, logsumexp=logsumexp, shared_keys=shared_keys, shared_values=shared_values, query_starts=query_starts, slab_starts=slab_starts)


def round_half(values_in):
    rounded = values_in.astype(jnp.bfloat16)
    rounded = lax.optimization_barrier(rounded)
    return rounded.astype(jnp.float32)


def reference(queries, out_grads, logsumexp, shared_keys, shared_values, query_starts, slab_starts):
    score_scale = HEAD_DIM ** -0.5
    group_size = Q_HEADS // KV_HEADS
    query_pos = (query_starts[:, None] + jnp.arange(QDEV, dtype=jnp.int32)[None, :]).astype(jnp.int32)
    key_pos = (slab_starts[:, None] + jnp.arange(SLAB, dtype=jnp.int32)[None, :]).reshape(-1).astype(jnp.int32)
    key_grads = jnp.zeros((KTOT, KV_HEADS * HEAD_DIM), jnp.float32)
    value_grads = jnp.zeros((KTOT, KV_HEADS * HEAD_DIM), jnp.float32)
    layer_grads = []
    for layer_index in range(LAYERS):
        query_all = queries[layer_index].astype(jnp.float32).reshape(SLABS, QDEV, Q_HEADS, HEAD_DIM)
        grad_all = out_grads[layer_index].astype(jnp.float32).reshape(SLABS, QDEV, Q_HEADS, HEAD_DIM)
        saved_all = jnp.transpose(logsumexp[layer_index].reshape(Q_HEADS, SLABS, QDEV), (1, 0, 2))
        query_cols = []
        key_cols = []
        value_cols = []
        for head_index in range(KV_HEADS):
            low = head_index * group_size
            key_head = shared_keys[:, head_index * HEAD_DIM:(head_index + 1) * HEAD_DIM].astype(jnp.float32)
            value_head = shared_values[:, head_index * HEAD_DIM:(head_index + 1) * HEAD_DIM].astype(jnp.float32)

            def block_step(packed):
                query_group, grad_group, saved, rows_pos = packed
                visible = key_pos[None, :] <= rows_pos[:, None]
                scores = jnp.einsum('rhd,kd->hrk', query_group, key_head) * score_scale
                probs = jnp.where(visible[None], jnp.exp(scores - saved[:, :, None]), 0.0)
                grad_probs = jnp.einsum('rhd,kd->hrk', grad_group, value_head)
                row_delta = jnp.sum(probs * grad_probs, axis=2, keepdims=True)
                grad_scores = probs * (grad_probs - row_delta)
                probs_half = round_half(probs)
                scores_half = round_half(grad_scores)
                value_piece = jnp.einsum('hrk,rhd->kd', probs_half, grad_group)
                key_piece = jnp.einsum('hrk,rhd->kd', scores_half, query_group) * score_scale
                query_piece = (jnp.einsum('hrk,kd->rhd', scores_half, key_head) * score_scale).reshape(QDEV, group_size * HEAD_DIM)
                return query_piece, key_piece, value_piece

            query_blocks, key_blocks, value_blocks = lax.map(block_step, (query_all[:, :, low:low + group_size], grad_all[:, :, low:low + group_size], saved_all[:, low:low + group_size], query_pos))
            query_cols.append(query_blocks.reshape(QTOT, group_size * HEAD_DIM))
            key_cols.append(jnp.sum(key_blocks, axis=0))
            value_cols.append(jnp.sum(value_blocks, axis=0))
        layer_grads.append(jnp.concatenate(query_cols, axis=1))
        key_grads = key_grads + jnp.concatenate(key_cols, axis=1)
        value_grads = value_grads + jnp.concatenate(value_cols, axis=1)
    return jnp.stack(layer_grads), key_grads, value_grads
```

```python
import jax
import jax.numpy as jnp
from jax import lax
from jax.experimental import pallas as pl
from jax.experimental.pallas import tpu as pltpu
from jax.sharding import Mesh
from jax.sharding import PartitionSpec as P

KV_HEADS = 8
GROUP = 3
HEAD_DIM = 128
ROWS = 256
SLAB = 16
SCALE = HEAD_DIM**-0.5
LOG2E = 1.4426950408889634
WIDE = GROUP * ROWS
MINE = KV_HEADS // 2
COLS = MINE * HEAD_DIM
KEYS = 1024
BLOCK = 256
AXES = ("zl", "core", "zh", "x", "y")


def attention_kernel(
    meta, q_own, g_own, lse_own, q_oth, g_oth, lse_oth, kv0, kv1, kv2, kv3,
    dq_own, dq_oth, out0, out1, out2, out3,
    key_s, val_s, pos_s, rows_q, rows_g, prob_s, gp_s, half_s, ds_s, dk_s, dv_s,
):
    step = pl.program_id(0)
    core, a0, b0, z0, first = (meta[i] for i in range(5))
    a_step = jnp.where(core == 0, 1, 4)
    b_step = jnp.where(core == 0, 4, 1)

    @pl.when(step == 0)
    def _():
        row = lax.broadcasted_iota(jnp.int32, (SLAB, 128), 0).astype(jnp.float32)
        for a, piece in enumerate((kv0, kv1, kv2, kv3)):
            for b in range(4):
                for z in range(4):
                    slab = ((z0 - z) & 3) * 16 + ((a0 - a) & 3) * a_step + ((b0 - b) & 3) * b_step
                    src = pl.ds((b * 4 + z) * SLAB, SLAB)
                    dst = pl.ds(pl.multiple_of(slab * SLAB, SLAB), SLAB)
                    for h in range(MINE):
                        key_s[h, dst, :] = piece[src, h * 128:(h + 1) * 128]
                        val_s[h, dst, :] = piece[src, COLS + h * 128:COLS + (h + 1) * 128]
                    pos_s[dst, :] = (
                        piece[src, 2 * COLS:2 * COLS + 128].astype(jnp.float32)
                        + row + (slab * 256).astype(jnp.float32)
                    )

    lane = lax.broadcasted_iota(jnp.int32, (1, 128), 1)
    q_pos = [(first + lane + c * 128).astype(jnp.float32) for c in range(2)]

    for layer, (q_ref, g_ref, l_ref, dq_ref) in enumerate(
        ((q_own, g_own, lse_own, dq_own), (q_oth, g_oth, lse_oth, dq_oth))
    ):
        for h in range(GROUP):
            rows_q[layer, h * ROWS:(h + 1) * ROWS, :] = q_ref[:, h * 128:(h + 1) * 128]
            rows_g[layer, h * ROWS:(h + 1) * ROWS, :] = g_ref[:, h * 128:(h + 1) * 128]
        queries = rows_q[layer]
        grads = rows_g[layer]
        lse = l_ref[0] * LOG2E
        delta = jnp.zeros((1, WIDE), jnp.float32)
        for kb in range(KEYS // BLOCK):
            sl = slice(kb * BLOCK, (kb + 1) * BLOCK)
            score = lax.dot_general(
                key_s[step, sl, :], queries, (((1,), (1,)), ((), ())),
                preferred_element_type=jnp.float32,
            )
            prob = jnp.exp2(score * (SCALE * LOG2E) - lse)
            k_pos = pos_s[sl, :]
            seen = jnp.concatenate([k_pos <= q_pos[0], k_pos <= q_pos[1]] * GROUP, axis=1)
            prob = jnp.where(seen, prob, 0.0)
            grad_prob = lax.dot_general(
                val_s[step, sl, :], grads, (((1,), (1,)), ((), ())),
                preferred_element_type=jnp.float32,
            )
            delta = delta + jnp.sum(prob * grad_prob, axis=0, keepdims=True)
            prob_s[layer, sl, :] = prob
            gp_s[layer, sl, :] = grad_prob
            half_s[layer, sl, :] = prob.astype(jnp.bfloat16)
        for kb in range(KEYS // BLOCK):
            sl = slice(kb * BLOCK, (kb + 1) * BLOCK)
            ds_s[layer, sl, :] = (prob_s[layer, sl, :] * (gp_s[layer, sl, :] - delta)).astype(jnp.bfloat16)
        dv = jnp.dot(half_s[layer], grads, preferred_element_type=jnp.float32)
        dk = jnp.dot(ds_s[layer], queries, preferred_element_type=jnp.float32)
        if layer == 0:
            dv_s[...] = dv
            dk_s[...] = dk
        else:
            dv_s[...] += dv
            dk_s[...] = (dk_s[...] + dk) * SCALE
        dq_t = lax.dot_general(
            key_s[step], ds_s[layer], (((0,), (0,)), ((), ())),
            preferred_element_type=jnp.float32,
        ) * SCALE
        for h in range(GROUP):
            dq_ref[:, h * 128:(h + 1) * 128] = dq_t[:, h * ROWS:(h + 1) * ROWS].T

    for a, out in enumerate((out0, out1, out2, out3)):
        for b in range(4):
            for z in range(4):
                slab = z * 16 + ((a0 + a) & 3) * a_step + ((b0 + b) & 3) * b_step
                src = pl.ds(pl.multiple_of(slab * SLAB, SLAB), SLAB)
                dst = pl.ds((b * 4 + z) * SLAB, SLAB)
                out[0, dst, :] = dk_s[src, :].astype(out.dtype)
                out[1, dst, :] = dv_s[src, :].astype(out.dtype)


def attention(meta, q_own, g_own, lse_own, q_oth, g_oth, lse_oth, kv):
    def head(g, m):
        return (g // 2) * 4 + m[0] * 2 + g % 2

    f32, bf16 = jnp.float32, jnp.bfloat16
    width = GROUP * HEAD_DIM
    own = pl.BlockSpec((ROWS, width), lambda g, m: (0, head(g, m)))
    oth = pl.BlockSpec((ROWS, width), lambda g, m: (0, g))
    part = pl.BlockSpec((BLOCK, kv[0].shape[1]), lambda g, m: (0, 0))
    out = pl.BlockSpec((2, BLOCK, HEAD_DIM), lambda g, m: (0, 0, g))
    return pl.pallas_call(
        attention_kernel,
        grid_spec=pltpu.PrefetchScalarGridSpec(
            num_scalar_prefetch=1,
            grid=(MINE,),
            in_specs=[
                own, own, pl.BlockSpec((1, 1, WIDE), lambda g, m: (head(g, m), 0, 0)),
                oth, oth, pl.BlockSpec((1, 1, WIDE), lambda g, m: (g, 0, 0)),
                part, part, part, part,
            ],
            out_specs=[own, oth, out, out, out, out],
            scratch_shapes=[
                pltpu.VMEM((MINE, KEYS, HEAD_DIM), bf16),
                pltpu.VMEM((MINE, KEYS, HEAD_DIM), bf16),
                pltpu.VMEM((KEYS, 128), f32),
                pltpu.VMEM((2, WIDE, HEAD_DIM), bf16),
                pltpu.VMEM((2, WIDE, HEAD_DIM), bf16),
                pltpu.VMEM((2, KEYS, WIDE), f32),
                pltpu.VMEM((2, KEYS, WIDE), f32),
                pltpu.VMEM((2, KEYS, WIDE), bf16),
                pltpu.VMEM((2, KEYS, WIDE), bf16),
                pltpu.VMEM((KEYS, HEAD_DIM), f32),
                pltpu.VMEM((KEYS, HEAD_DIM), f32),
            ],
        ),
        out_shape=[
            jax.ShapeDtypeStruct((ROWS, KV_HEADS * width), f32),
            jax.ShapeDtypeStruct((ROWS, MINE * width), f32),
            jax.ShapeDtypeStruct((2, BLOCK, COLS), f32),
        ] + [jax.ShapeDtypeStruct((2, BLOCK, COLS), bf16)] * 3,
        compiler_params=pltpu.CompilerParams(vmem_limit_bytes=50 * 2**20),
        cost_estimate=pl.CostEstimate(
            flops=8 * 10**9, bytes_accessed=16 * 2**20, transcendentals=6 * 10**6
        ),
        name="attention_backward",
    )(meta, q_own, g_own, lse_own, q_oth, g_oth, lse_oth, *kv)


def shift(value, axis, by):
    return lax.ppermute(value, axis, [(i, (i + by) % 4) for i in range(4)])


def plane_shift(value, by, x_core):
    pairs = []
    for core in range(2):
        for x in range(4):
            for y in range(4):
                to = ((x + by) % 4, y) if core == x_core else (x, (y + by) % 4)
                pairs.append((core * 16 + x * 4 + y, core * 16 + to[0] * 4 + to[1]))
    return lax.ppermute(value, ("core", "x", "y"), pairs)


def swap(value):
    return lax.ppermute(value, "core", [(0, 1), (1, 0)])


def per_device(
    queries, out_grads, logsumexp, shared_keys, shared_values, query_starts, slab_starts
):
    core, zh, x, y = (lax.axis_index(n) for n in ("core", "zh", "x", "y"))
    other = 1 - core
    seq = zh * 16 + x * 4 + y
    queries, out_grads = queries[0], out_grads[0]

    def halves(value, which, width, axis=1):
        return jnp.concatenate(
            [
                lax.dynamic_slice_in_dim(value, which * width, width, axis),
                lax.dynamic_slice_in_dim(value, (2 + which) * width, width, axis),
            ],
            axis,
        )

    with jax.named_scope("gather_keys"):
        offset = (slab_starts[0] - seq * 256).astype(jnp.bfloat16)
        payload = jnp.concatenate(
            [
                halves(shared_keys, core, 256),
                halves(shared_values, core, 256),
                jnp.broadcast_to(offset, (SLAB, 128)),
            ],
            1,
        )
        block = jnp.concatenate([payload] + [shift(payload, "zh", r) for r in (1, 2, 3)], 0)
    with jax.named_scope("swap_queries"):
        lse = logsumexp[0].reshape(KV_HEADS, WIDE)
        q_oth = swap(halves(queries, other, 768))
        g_oth = swap(halves(out_grads, other, 768))
        lse_oth = swap(halves(lse, other, 2, 0))
    with jax.named_scope("gather_keys"):
        block = jnp.concatenate([block] + [plane_shift(block, r, 0) for r in (1, 2, 3)], 0)
        pieces = [block] + [plane_shift(block, r, 1) for r in (1, 2, 3)]

    a0 = jnp.where(core == 0, y, x)
    b0 = jnp.where(core == 0, x, y)
    meta = jnp.stack([core, a0, b0, zh, query_starts[0]]).astype(jnp.int32)
    dq, dq_oth, part0, *parts = attention(
        meta, queries, out_grads, lse[:, None], q_oth, g_oth, lse_oth[:, None], pieces
    )

    with jax.named_scope("scatter_grads"):
        total = part0
        for r, part in enumerate(parts):
            total = total + plane_shift(part, r + 1, 1).astype(jnp.float32)
    with jax.named_scope("swap_query_grads"):
        back = swap(dq_oth)
        dq = lax.dynamic_update_slice(dq, back[:, :768], (0, other * 768))
        dq = lax.dynamic_update_slice(dq, back[:, 768:], (0, (2 + other) * 768))
    with jax.named_scope("scatter_grads"):
        small = total[:, :64]
        for r in (1, 2, 3):
            piece = total[:, r * 64:(r + 1) * 64].astype(jnp.bfloat16)
            small = small + plane_shift(piece, r, 0).astype(jnp.float32)
        small = small.reshape(2, 4, SLAB, 2, 256).transpose(3, 1, 0, 2, 4).reshape(8, 2, SLAB, 256)
        got = lax.all_to_all(small, ("zl", "zh"), 0, 0)
        grads = jnp.sum(got, 0)
    return dq[None], grads[0], grads[1]


def solution(mesh):
    fine = Mesh(mesh.devices.reshape(2, 2, 4, 4, 4), AXES)
    section, seq = ("zl", "core"), ("zh", "x", "y")
    return jax.shard_map(
        per_device,
        mesh=fine,
        in_specs=(
            P(section, seq, None),
            P(section, seq, None),
            P(section, None, seq),
            P(seq, None),
            P(seq, None),
            P(seq),
            P(seq),
        ),
        out_specs=(P(section, seq, None), P(seq, section), P(seq, section)),
        check_vma=False,
    )
```

```python
import jax
import jax.numpy as jnp
from jax import lax
from jax.experimental import pallas as pl
from jax.experimental.pallas import tpu as pltpu
from jax.sharding import Mesh
from jax.sharding import PartitionSpec as P

KV_HEADS = 8
GROUP = 3
HEAD_DIM = 128
ROWS = 256
SLAB = 16
SCALE = HEAD_DIM**-0.5
LOG2E = 1.4426950408889634
WIDE = GROUP * ROWS
MINE = KV_HEADS // 2
COLS = MINE * HEAD_DIM
KEYS = 1024
BLOCK = 256
AXES = ("zl", "core", "zh", "x", "y")


def attention_kernel(
    meta, q_own, g_own, lse_own, q_oth, g_oth, lse_oth, kv0, kv1, kv2, kv3,
    dq_own, dq_oth, out0, out1, out2, out3,
    key_s, val_s, pos_s, rows_q, rows_g, prob_s, gp_s, half_s, ds_s, dk_s, dv_s,
):
    step = pl.program_id(0)
    core, a0, first = (meta[i] for i in range(3))
    a_step = jnp.where(core == 0, 1, 4)
    b_step = jnp.where(core == 0, 4, 1)

    @pl.when(step == 0)
    def _():
        row = lax.broadcasted_iota(jnp.int32, (SLAB, 128), 0).astype(jnp.float32)
        for a, piece in enumerate((kv0, kv1, kv2, kv3)):
            for b in range(4):
                for z in range(4):
                    slab = z * 16 + ((a0 - a) & 3) * a_step + b * b_step
                    src = pl.ds((b * 4 + z) * SLAB, SLAB)
                    dst = pl.ds(pl.multiple_of(slab * SLAB, SLAB), SLAB)
                    for h in range(MINE):
                        key_s[h, dst, :] = piece[src, h * 128:(h + 1) * 128]
                        val_s[h, dst, :] = piece[src, COLS + h * 128:COLS + (h + 1) * 128]
                    pos_s[dst, :] = (
                        piece[src, 2 * COLS:2 * COLS + 128].astype(jnp.float32)
                        + row + (slab * 256).astype(jnp.float32)
                    )

    lane = lax.broadcasted_iota(jnp.int32, (1, 128), 1)
    q_pos = [(first + lane + c * 128).astype(jnp.float32) for c in range(2)]

    for layer, (q_ref, g_ref, l_ref, dq_ref) in enumerate(
        ((q_own, g_own, lse_own, dq_own), (q_oth, g_oth, lse_oth, dq_oth))
    ):
        for h in range(GROUP):
            rows_q[layer, h * ROWS:(h + 1) * ROWS, :] = q_ref[:, h * 128:(h + 1) * 128]
            rows_g[layer, h * ROWS:(h + 1) * ROWS, :] = g_ref[:, h * 128:(h + 1) * 128]
        queries = rows_q[layer]
        grads = rows_g[layer]
        lse = l_ref[0] * LOG2E
        delta = jnp.zeros((1, WIDE), jnp.float32)
        for kb in range(KEYS // BLOCK):
            sl = slice(kb * BLOCK, (kb + 1) * BLOCK)
            score = lax.dot_general(
                key_s[step, sl, :], queries, (((1,), (1,)), ((), ())),
                preferred_element_type=jnp.float32,
            )
            prob = jnp.exp2(score * (SCALE * LOG2E) - lse)
            k_pos = pos_s[sl, :]
            seen = jnp.concatenate([k_pos <= q_pos[0], k_pos <= q_pos[1]] * GROUP, axis=1)
            prob = jnp.where(seen, prob, 0.0)
            grad_prob = lax.dot_general(
                val_s[step, sl, :], grads, (((1,), (1,)), ((), ())),
                preferred_element_type=jnp.float32,
            )
            delta = delta + jnp.sum(prob * grad_prob, axis=0, keepdims=True)
            prob_s[layer, sl, :] = prob
            gp_s[layer, sl, :] = grad_prob
            half_s[layer, sl, :] = prob.astype(jnp.bfloat16)
        for kb in range(KEYS // BLOCK):
            sl = slice(kb * BLOCK, (kb + 1) * BLOCK)
            ds_s[layer, sl, :] = (prob_s[layer, sl, :] * (gp_s[layer, sl, :] - delta)).astype(jnp.bfloat16)
        dv = jnp.dot(half_s[layer], grads, preferred_element_type=jnp.float32)
        dk = jnp.dot(ds_s[layer], queries, preferred_element_type=jnp.float32)
        if layer == 0:
            dv_s[...] = dv
            dk_s[...] = dk
        else:
            dv_s[...] += dv
            dk_s[...] = (dk_s[...] + dk) * SCALE
        dq_t = lax.dot_general(
            key_s[step], ds_s[layer], (((0,), (0,)), ((), ())),
            preferred_element_type=jnp.float32,
        ) * SCALE
        for h in range(GROUP):
            dq_ref[:, h * 128:(h + 1) * 128] = dq_t[:, h * ROWS:(h + 1) * ROWS].T

    for a, out in enumerate((out0, out1, out2, out3)):
        for b in range(4):
            for z in range(4):
                slab = z * 16 + ((a0 + a) & 3) * a_step + b * b_step
                src = pl.ds(pl.multiple_of(slab * SLAB, SLAB), SLAB)
                out[b, 0, z, 0] = dk_s[src, :].astype(out.dtype)
                out[b, 0, z, 1] = dv_s[src, :].astype(out.dtype)


def attention(meta, q_own, g_own, lse_own, q_oth, g_oth, lse_oth, kv):
    def head(g, m):
        return (g // 2) * 4 + m[0] * 2 + g % 2

    f32, bf16 = jnp.float32, jnp.bfloat16
    width = GROUP * HEAD_DIM
    own = pl.BlockSpec((ROWS, width), lambda g, m: (0, head(g, m)))
    back = pl.BlockSpec((ROWS, width), lambda g, m: (0, g))
    part = pl.BlockSpec((BLOCK, kv[0].shape[1]), lambda g, m: (0, 0))
    lse = pl.BlockSpec((1, 1, WIDE), lambda g, m: (head(g, m), 0, 0))
    out_dims = (4, 2, 4, 2, SLAB, 2 * HEAD_DIM)
    out = pl.BlockSpec(
        (4, 1, 4, 2, SLAB, HEAD_DIM), lambda g, m: (0, g // 2, 0, 0, 0, g % 2)
    )
    return pl.pallas_call(
        attention_kernel,
        grid_spec=pltpu.PrefetchScalarGridSpec(
            num_scalar_prefetch=1,
            grid=(MINE,),
            in_specs=[own, own, lse, own, own, lse, part, part, part, part],
            out_specs=[own, back, out, out, out, out],
            scratch_shapes=[
                pltpu.VMEM((MINE, KEYS, HEAD_DIM), bf16),
                pltpu.VMEM((MINE, KEYS, HEAD_DIM), bf16),
                pltpu.VMEM((KEYS, 128), f32),
                pltpu.VMEM((2, WIDE, HEAD_DIM), bf16),
                pltpu.VMEM((2, WIDE, HEAD_DIM), bf16),
                pltpu.VMEM((2, KEYS, WIDE), f32),
                pltpu.VMEM((2, KEYS, WIDE), f32),
                pltpu.VMEM((2, KEYS, WIDE), bf16),
                pltpu.VMEM((2, KEYS, WIDE), bf16),
                pltpu.VMEM((KEYS, HEAD_DIM), f32),
                pltpu.VMEM((KEYS, HEAD_DIM), f32),
            ],
        ),
        out_shape=[
            jax.ShapeDtypeStruct((ROWS, KV_HEADS * width), f32),
            jax.ShapeDtypeStruct((ROWS, MINE * width), f32),
            jax.ShapeDtypeStruct(out_dims, f32),
        ] + [jax.ShapeDtypeStruct(out_dims, bf16)] * 3,
        compiler_params=pltpu.CompilerParams(vmem_limit_bytes=50 * 2**20),
        cost_estimate=pl.CostEstimate(
            flops=8 * 10**9, bytes_accessed=16 * 2**20, transcendentals=6 * 10**6
        ),
        name="attention_backward",
    )(meta, q_own, g_own, lse_own, q_oth, g_oth, lse_oth, *kv)


def pack_kernel(meta, keys, values, out):
    core, offset = meta[0], meta[1]
    tail = jnp.full((SLAB, 128), offset, jnp.int32).astype(jnp.float32).astype(jnp.bfloat16)
    cols = [pl.ds(pl.multiple_of(n * 512 + core * 256, 128), 256) for n in range(2)]
    for to in range(4):
        for n in range(2):
            out[to, :, n * 256:(n + 1) * 256] = keys[:, cols[n]]
            out[to, :, COLS + n * 256:COLS + (n + 1) * 256] = values[:, cols[n]]
        out[to, :, 2 * COLS:] = tail


def pack(meta, keys, values):
    return pl.pallas_call(
        pack_kernel,
        in_specs=[
            pl.BlockSpec(memory_space=pltpu.SMEM),
            pl.BlockSpec(memory_space=pltpu.VMEM),
            pl.BlockSpec(memory_space=pltpu.VMEM),
        ],
        out_specs=pl.BlockSpec(memory_space=pltpu.VMEM),
        out_shape=jax.ShapeDtypeStruct((4, SLAB, 2 * COLS + 128), jnp.bfloat16),
        name="pack_keys_values",
    )(meta, keys, values)


def finish_kernel(got, dk, dv):
    for n, out in enumerate((dk, dv)):
        total = got[0, n].astype(jnp.float32)
        for i in range(1, 8):
            total = total + got[i, n].astype(jnp.float32)
        out[...] = total


def finish(got):
    shape = jax.ShapeDtypeStruct((SLAB, 2 * HEAD_DIM), jnp.float32)
    return pl.pallas_call(finish_kernel, out_shape=[shape, shape], name="add_last")(got)


def plane_shift(value, by, x_core):
    pairs = []
    for core in range(2):
        for x in range(4):
            for y in range(4):
                to = ((x + by) % 4, y) if core == x_core else (x, (y + by) % 4)
                pairs.append((core * 16 + x * 4 + y, core * 16 + to[0] * 4 + to[1]))
    return lax.ppermute(value, ("core", "x", "y"), pairs)


def plane_exchange(value, x_core):
    groups = []
    for core in range(2):
        for line in range(4):
            if core == x_core:
                groups.append([core * 16 + i * 4 + line for i in range(4)])
            else:
                groups.append([core * 16 + line * 4 + i for i in range(4)])
    return lax.all_to_all(value, ("core", "x", "y"), 0, 0, axis_index_groups=groups)


def add(terms):
    total = terms[0].astype(jnp.float32)
    for term in terms[1:]:
        total = total + term.astype(jnp.float32)
    return total.astype(jnp.bfloat16)


def swap(value):
    return lax.ppermute(value, "core", [(0, 1), (1, 0)])


def per_device(
    queries, out_grads, logsumexp, shared_keys, shared_values, query_starts, slab_starts
):
    core, zh, x, y = (lax.axis_index(n) for n in ("core", "zh", "x", "y"))
    other = 1 - core
    seq = zh * 16 + x * 4 + y
    queries, out_grads, lse = queries[0], out_grads[0], logsumexp[0]

    with jax.named_scope("gather_keys"):
        offset = slab_starts[0] - seq * 256
        payload = pack(jnp.stack([core, offset]).astype(jnp.int32), shared_keys, shared_values)
        block = lax.all_to_all(payload, "zh", 0, 0)
        block = plane_exchange(jnp.broadcast_to(block, (4, *block.shape)), 0)
        block = block.reshape(BLOCK, 2 * COLS + 128)
        pieces = [block] + [plane_shift(block, r, 1) for r in (1, 2, 3)]
    with jax.named_scope("swap_queries"):
        q_oth, g_oth, lse_oth = (swap(v) for v in (queries, out_grads, lse))

    a0 = jnp.where(core == 0, y, x)
    meta = jnp.stack([core, a0, query_starts[0]]).astype(jnp.int32)
    wide = (KV_HEADS, 1, WIDE)
    dq, dq_oth, part0, *parts = attention(
        meta, queries, out_grads, lse.reshape(wide), q_oth, g_oth, lse_oth.reshape(wide), pieces
    )

    with jax.named_scope("scatter_grads"):
        parts = [plane_shift(part, r + 1, 1) for r, part in enumerate(parts)]
    with jax.named_scope("swap_query_grads"):
        back = swap(dq_oth)
        dq = lax.dynamic_update_slice(dq, back[:, :768], (0, other * 768))
        dq = lax.dynamic_update_slice(dq, back[:, 768:], (0, (2 + other) * 768))
    with jax.named_scope("scatter_grads"):
        parts[0], dq = lax.optimization_barrier((parts[0], dq))
        got = plane_exchange(add([part0, *parts]), 0)
        small = add([got[i] for i in range(4)]).reshape(8, 2, SLAB, 2 * HEAD_DIM)
        dk, dv = finish(lax.all_to_all(small, ("zl", "zh"), 0, 0))
    return dq[None], dk, dv


def solution(mesh):
    fine = Mesh(mesh.devices.reshape(2, 2, 4, 4, 4), AXES)
    section, seq = ("zl", "core"), ("zh", "x", "y")
    return jax.shard_map(
        per_device,
        mesh=fine,
        in_specs=(
            P(section, seq, None),
            P(section, seq, None),
            P(section, None, seq),
            P(seq, None),
            P(seq, None),
            P(seq),
            P(seq),
        ),
        out_specs=(P(section, seq, None), P(seq, section), P(seq, section)),
        check_vma=False,
    )
```

```python
import jax
import jax.numpy as jnp
from jax import lax
from jax.experimental import pallas as pl
from jax.experimental.pallas import tpu as pltpu
from jax.sharding import Mesh
from jax.sharding import PartitionSpec as P

KV_HEADS = 8
GROUP = 3
HEAD_DIM = 128
ROWS = 256
SLAB = 16
SCALE = HEAD_DIM**-0.5
LOG2E = 1.4426950408889634
WIDE = GROUP * ROWS
PAIR = 2
COLS = PAIR * HEAD_DIM
PAYLOAD = 2 * COLS + 128
KEYS = 1024
BLOCK = 256
AXES = ("zl", "core", "zh", "x", "y")


SMALL = pltpu.CompilerParams(vmem_limit_bytes=8 * 2**20)


def attention_kernel(
    meta, q_own, g_own, lse_own, q_oth, g_oth, lse_oth, kv0, kv1, kv2, kv3, *rest
):
    (
        dq_own, dq_oth, out0, out1, out2, out3,
        key_s, val_s, pos_s, rows_q, rows_g, prob_s, gp_s, half_s, ds_s, dk_s, dv_s,
    ) = rest[-17:]
    step = pl.program_id(0)
    core, a0, first = (meta[i] for i in range(3))
    a_step = jnp.where(core == 0, 1, 4)
    b_step = jnp.where(core == 0, 4, 1)

    @pl.when(step == 0)
    def _():
        row = lax.broadcasted_iota(jnp.int32, (SLAB, 128), 0).astype(jnp.float32)
        for a, piece in enumerate((kv0, kv1, kv2, kv3)):
            for b in range(4):
                for z in range(4):
                    slab = z * 16 + ((a0 - a) & 3) * a_step + b * b_step
                    src = pl.ds((b * 4 + z) * SLAB, SLAB)
                    dst = pl.ds(pl.multiple_of(slab * SLAB, SLAB), SLAB)
                    for h in range(PAIR):
                        key_s[h, dst, :] = piece[src, h * 128:(h + 1) * 128]
                        val_s[h, dst, :] = piece[src, COLS + h * 128:COLS + (h + 1) * 128]
                    pos_s[dst, :] = (
                        piece[src, 2 * COLS:2 * COLS + 128].astype(jnp.float32)
                        + row + (slab * 256).astype(jnp.float32)
                    )

    lane = lax.broadcasted_iota(jnp.int32, (1, 128), 1)
    q_pos = [(first + lane + c * 128).astype(jnp.float32) for c in range(2)]

    for layer, (q_ref, g_ref, l_ref, dq_ref) in enumerate(
        ((q_own, g_own, lse_own, dq_own), (q_oth, g_oth, lse_oth, dq_oth))
    ):
        for h in range(GROUP):
            rows_q[layer, h * ROWS:(h + 1) * ROWS, :] = q_ref[:, h * 128:(h + 1) * 128]
            rows_g[layer, h * ROWS:(h + 1) * ROWS, :] = g_ref[:, h * 128:(h + 1) * 128]
        queries = rows_q[layer]
        grads = rows_g[layer]
        lse = l_ref[0] * LOG2E
        delta = jnp.zeros((1, WIDE), jnp.float32)
        for kb in range(KEYS // BLOCK):
            sl = slice(kb * BLOCK, (kb + 1) * BLOCK)
            score = lax.dot_general(
                key_s[step, sl, :], queries, (((1,), (1,)), ((), ())),
                preferred_element_type=jnp.float32,
            )
            prob = jnp.exp2(score * (SCALE * LOG2E) - lse)
            k_pos = pos_s[sl, :]
            seen = jnp.concatenate([k_pos <= q_pos[0], k_pos <= q_pos[1]] * GROUP, axis=1)
            prob = jnp.where(seen, prob, 0.0)
            grad_prob = lax.dot_general(
                val_s[step, sl, :], grads, (((1,), (1,)), ((), ())),
                preferred_element_type=jnp.float32,
            )
            delta = delta + jnp.sum(prob * grad_prob, axis=0, keepdims=True)
            prob_s[layer, sl, :] = prob
            gp_s[layer, sl, :] = grad_prob
            half_s[layer, sl, :] = prob.astype(jnp.bfloat16)
        for kb in range(KEYS // BLOCK):
            sl = slice(kb * BLOCK, (kb + 1) * BLOCK)
            ds_s[layer, sl, :] = (prob_s[layer, sl, :] * (gp_s[layer, sl, :] - delta)).astype(jnp.bfloat16)
        dv = jnp.dot(half_s[layer], grads, preferred_element_type=jnp.float32)
        dk = jnp.dot(ds_s[layer], queries, preferred_element_type=jnp.float32)
        if layer == 0:
            dv_s[...] = dv
            dk_s[...] = dk
        else:
            dv_s[...] += dv
            dk_s[...] = (dk_s[...] + dk) * SCALE
        dq_t = lax.dot_general(
            key_s[step], ds_s[layer], (((0,), (0,)), ((), ())),
            preferred_element_type=jnp.float32,
        ) * SCALE
        for h in range(GROUP):
            dq_ref[:, h * 128:(h + 1) * 128] = dq_t[:, h * ROWS:(h + 1) * ROWS].T

    for a, out in enumerate((out0, out1, out2, out3)):
        for b in range(4):
            for z in range(4):
                slab = z * 16 + ((a0 + a) & 3) * a_step + b * b_step
                src = pl.ds(pl.multiple_of(slab * SLAB, SLAB), SLAB)
                out[b, z, 0] = dk_s[src, :].astype(out.dtype)
                out[b, z, 1] = dv_s[src, :].astype(out.dtype)


def attention(chunk, meta, q_own, g_own, lse_own, q_oth, g_oth, lse_oth, kv, partly):
    def head(g, m):
        return chunk * 4 + m[0] * 2 + g

    q_own, g_own, q_oth, g_oth = (
        pltpu.with_memory_space_constraint(v, pltpu.HBM) for v in (q_own, g_own, q_oth, g_oth)
    )
    f32, bf16 = jnp.float32, jnp.bfloat16
    width = GROUP * HEAD_DIM
    own = pl.BlockSpec((ROWS, width), lambda g, m: (0, head(g, m)))
    back = pl.BlockSpec((ROWS, width), lambda g, m: (0, chunk * 2 + g))
    part = pl.BlockSpec((BLOCK, PAYLOAD), lambda g, m: (0, 0))
    lse = pl.BlockSpec((1, 1, WIDE), lambda g, m: (head(g, m), 0, 0))
    out_dims = (4, 4, 2, SLAB, PAIR * HEAD_DIM)
    out = pl.BlockSpec((4, 4, 2, SLAB, HEAD_DIM), lambda g, m: (0, 0, 0, 0, g))
    return pl.pallas_call(
        attention_kernel,
        grid_spec=pltpu.PrefetchScalarGridSpec(
            num_scalar_prefetch=1,
            grid=(PAIR,),
            in_specs=[own, own, lse, own, own, lse, part, part, part, part]
            + [pl.BlockSpec(memory_space=pl.ANY)] * len(partly),
            out_specs=[own, back, out, out, out, out],
            scratch_shapes=[
                pltpu.VMEM((PAIR, KEYS, HEAD_DIM), bf16),
                pltpu.VMEM((PAIR, KEYS, HEAD_DIM), bf16),
                pltpu.VMEM((KEYS, 128), f32),
                pltpu.VMEM((2, WIDE, HEAD_DIM), bf16),
                pltpu.VMEM((2, WIDE, HEAD_DIM), bf16),
                pltpu.VMEM((2, KEYS, WIDE), f32),
                pltpu.VMEM((2, KEYS, WIDE), f32),
                pltpu.VMEM((2, KEYS, WIDE), bf16),
                pltpu.VMEM((2, KEYS, WIDE), bf16),
                pltpu.VMEM((KEYS, HEAD_DIM), f32),
                pltpu.VMEM((KEYS, HEAD_DIM), f32),
            ],
        ),
        out_shape=[
            pltpu.HBM((ROWS, KV_HEADS * width), f32),
            pltpu.HBM((ROWS, KV_HEADS // 2 * width), f32),
            pltpu.HBM(out_dims, f32),
        ] + [pltpu.HBM(out_dims, bf16)] * 3,
        input_output_aliases={11 + n: n for n in range(len(partly))},
        compiler_params=pltpu.CompilerParams(vmem_limit_bytes=36 * 2**20),
        cost_estimate=pl.CostEstimate(
            flops=8 * 10**9, bytes_accessed=8 * 2**20, transcendentals=3 * 10**6
        ),
        name="attention_backward",
    )(meta, q_own, g_own, lse_own, q_oth, g_oth, lse_oth, *kv, *partly)


def pack_kernel(starts, keys, values, out):
    core, zh, x, y = (lax.axis_index(n) for n in ("core", "zh", "x", "y"))
    offset = starts[0] - (zh * 16 + x * 4 + y) * 256
    tail = jnp.full((SLAB, 128), offset, jnp.int32).astype(jnp.float32).astype(jnp.bfloat16)
    for chunk in range(2):
        cols = pl.ds(pl.multiple_of(chunk * 512 + core * COLS, 128), COLS)
        for to in range(4):
            out[to, chunk, :, :COLS] = keys[:, cols]
            out[to, chunk, :, COLS:2 * COLS] = values[:, cols]
            out[to, chunk, :, 2 * COLS:] = tail


def pack(starts, keys, values):
    keys, values = (pltpu.with_memory_space_constraint(v, pltpu.HBM) for v in (keys, values))
    return pl.pallas_call(
        pack_kernel,
        in_specs=[
            pl.BlockSpec(memory_space=pltpu.SMEM),
            pl.BlockSpec(memory_space=pltpu.VMEM),
            pl.BlockSpec(memory_space=pltpu.VMEM),
        ],
        out_specs=pl.BlockSpec(memory_space=pltpu.VMEM),
        out_shape=jax.ShapeDtypeStruct((4, 2, SLAB, PAYLOAD), jnp.bfloat16),
        compiler_params=SMALL,
        name="pack_keys_values",
    )(starts, keys, values)


def join_kernel(*refs):
    out = refs[-1]
    total = refs[0][...]
    for ref in refs[1:4]:
        total = total + ref[...].astype(jnp.float32)
    out[:, 0] = total.astype(jnp.bfloat16)


def join(chunk, terms, partly):
    dims = terms[0].shape
    whole = pl.BlockSpec(dims, lambda i: (0,) * 5)
    return pl.pallas_call(
        join_kernel,
        grid=(1,),
        in_specs=[whole] * 4 + [pl.BlockSpec(memory_space=pl.ANY)] * len(partly),
        out_specs=pl.BlockSpec((dims[0], 1, *dims[1:]), lambda i: (0, chunk, 0, 0, 0, 0)),
        out_shape=jax.ShapeDtypeStruct((dims[0], 2, *dims[1:]), jnp.bfloat16),
        input_output_aliases={4: 0} if partly else {},
        compiler_params=SMALL,
        name="add_first",
    )(*terms, *partly)


def finish_kernel(got, dk, dv):
    for n, out in enumerate((dk, dv)):
        total = got[0, n].astype(jnp.float32)
        for i in range(1, 8):
            total = total + got[i, n].astype(jnp.float32)
        out[...] = total


def finish(got):
    shape = jax.ShapeDtypeStruct((SLAB, 2 * HEAD_DIM), jnp.float32)
    return pl.pallas_call(finish_kernel, out_shape=[shape, shape], compiler_params=SMALL, name="add_last")(got)


def plane_shift(value, by, x_core):
    pairs = []
    for core in range(2):
        for x in range(4):
            for y in range(4):
                to = ((x + by) % 4, y) if core == x_core else (x, (y + by) % 4)
                pairs.append((core * 16 + x * 4 + y, core * 16 + to[0] * 4 + to[1]))
    return lax.ppermute(value, ("core", "x", "y"), pairs)


def plane_exchange(value, x_core):
    groups = []
    for core in range(2):
        for line in range(4):
            if core == x_core:
                groups.append([core * 16 + i * 4 + line for i in range(4)])
            else:
                groups.append([core * 16 + line * 4 + i for i in range(4)])
    return lax.all_to_all(value, ("core", "x", "y"), 0, 0, axis_index_groups=groups)


def add(terms):
    total = terms[0].astype(jnp.float32)
    for term in terms[1:]:
        total = total + term.astype(jnp.float32)
    return total.astype(jnp.bfloat16)


def swap(value):
    return lax.ppermute(value, "core", [(0, 1), (1, 0)])


def per_device(
    queries, out_grads, logsumexp, shared_keys, shared_values, query_starts, slab_starts
):
    core, x, y = (lax.axis_index(n) for n in ("core", "x", "y"))
    other = 1 - core
    queries, out_grads, lse = queries[0], out_grads[0], logsumexp[0]

    with jax.named_scope("gather_keys"):
        payload = pack(slab_starts, shared_keys, shared_values)
        block = lax.all_to_all(payload, "zh", 0, 0)
        block = plane_exchange(jnp.broadcast_to(block, (4, *block.shape)), 0)
        pieces = []
        for chunk in range(2):
            piece = block[:, :, chunk].reshape(BLOCK, PAYLOAD)
            pieces.append([piece] + [plane_shift(piece, r, 1) for r in (1, 2, 3)])
    with jax.named_scope("swap_queries"):
        q_oth, g_oth, lse_oth = (swap(v) for v in (queries, out_grads, lse))

    a0 = jnp.where(core == 0, y, x)
    meta = jnp.stack([core, a0, query_starts[0]]).astype(jnp.int32)
    wide = (KV_HEADS, 1, WIDE)
    lse, lse_oth = lse.reshape(wide), lse_oth.reshape(wide)
    partly, sums = [], []
    for chunk in range(2):
        *partly, part0, part1, part2, part3 = attention(
            chunk, meta, queries, out_grads, lse, q_oth, g_oth, lse_oth, pieces[chunk], partly
        )
        with jax.named_scope("scatter_grads"):
            if sums:
                part0, part1, part2, part3, partly, sums = lax.optimization_barrier(
                    (part0, part1, part2, part3, partly, sums)
                )
            parts = [plane_shift(p, r, 1) for r, p in ((1, part1), (2, part2), (3, part3))]
        sums.append([part0, *parts])

    dq, dq_oth = partly
    with jax.named_scope("swap_query_grads"):
        back = swap(dq_oth)
        dq = lax.dynamic_update_slice(dq, back[:, :768], (0, other * 768))
        dq = lax.dynamic_update_slice(dq, back[:, 768:], (0, (2 + other) * 768))
    with jax.named_scope("scatter_grads"):
        sums[1][1], dq = lax.optimization_barrier((sums[1][1], dq))
        total = join(0, sums[0], [])
        total = join(1, sums[1], [total])
        got = plane_exchange(total, 0)
        small = add([got[i] for i in range(4)]).reshape(8, 2, SLAB, 2 * HEAD_DIM)
        dk, dv = finish(lax.all_to_all(small, ("zl", "zh"), 0, 0))
    return dq[None], dk, dv


def solution(mesh):
    fine = Mesh(mesh.devices.reshape(2, 2, 4, 4, 4), AXES)
    section, seq = ("zl", "core"), ("zh", "x", "y")
    return jax.shard_map(
        per_device,
        mesh=fine,
        in_specs=(
            P(section, seq, None),
            P(section, seq, None),
            P(section, None, seq),
            P(seq, None),
            P(seq, None),
            P(seq),
            P(seq),
        ),
        out_specs=(P(section, seq, None), P(seq, section), P(seq, section)),
        check_vma=False,
    )
```

```python
import jax
import jax.numpy as jnp
from jax import lax
from jax.experimental import pallas as pl
from jax.experimental.pallas import tpu as pltpu
from jax.sharding import Mesh
from jax.sharding import PartitionSpec as P

KV_HEADS = 8
GROUP = 3
HEAD_DIM = 128
ROWS = 256
SLAB = 16
SCALE = HEAD_DIM**-0.5
LOG2E = 1.4426950408889634
WIDE = GROUP * ROWS
PAIR = 2
COLS = PAIR * HEAD_DIM
PAYLOAD = 2 * COLS + 128
BLOCK = 256
APART = (0, 2, 1, 3)
AXES = ("zl", "core", "zh", "x", "y")


SMALL = pltpu.CompilerParams(vmem_limit_bytes=8 * 2**20)


def matmul(left, right, contract):
    return lax.dot_general(
        left, right, ((contract[:1], contract[1:]), ((), ())), preferred_element_type=jnp.float32
    )


def attention_kernel(
    meta, q_own, g_own, lse_own, q_oth, g_oth, lse_oth, kv0, kv1, kv2, kv3, *rest
):
    (
        dq_own, dq_oth, out0, out1, out2, out3,
        pos_s, key_s, val_s, rows_q, rows_g, prob_s, gp_s, half_s, ds_s,
    ) = rest[-15:]
    step = pl.program_id(0)
    core, a0, first = (meta[i] for i in range(3))
    pieces = (kv0, kv1, kv2, kv3)
    outs = (out0, out1, out2, out3)

    @pl.when(step == 0)
    def _():
        a_step = jnp.where(core == 0, 1, 4)
        b_step = jnp.where(core == 0, 4, 1)
        row = lax.broadcasted_iota(jnp.int32, (BLOCK, 128), 0)
        base = (((row >> 4) & 3) * 16 + (row >> 6) * b_step) * 256 + (row & 15)
        for a, piece in enumerate(pieces):
            slab = (a0 ^ APART[a]) * a_step
            pos_s[a] = piece[:, 2 * COLS:].astype(jnp.float32) + (base + slab * 256).astype(jnp.float32)
            for h in range(PAIR):
                key_s[h, a] = piece[:, h * 128:(h + 1) * 128]
                val_s[h, a] = piece[:, COLS + h * 128:COLS + (h + 1) * 128]

    lane = lax.broadcasted_iota(jnp.int32, (1, 128), 1)
    q_pos = [(first + lane + c * 128).astype(jnp.float32) for c in range(2)]
    sides = ((q_own, g_own, lse_own, dq_own), (q_oth, g_oth, lse_oth, dq_oth))

    for layer, (q_ref, g_ref, _, _) in enumerate(sides):
        for h in range(GROUP):
            rows = slice(layer * WIDE + h * ROWS, layer * WIDE + (h + 1) * ROWS)
            rows_q[rows, :] = q_ref[:, h * 128:(h + 1) * 128]
            rows_g[rows, :] = g_ref[:, h * 128:(h + 1) * 128]

    for layer, (_, _, lse_ref, _) in enumerate(sides):
        rows = slice(layer * WIDE, (layer + 1) * WIDE)
        lse = lse_ref[0] * LOG2E
        delta = jnp.zeros((1, WIDE), jnp.float32)
        for a in range(4):
            score = matmul(key_s[step, a], rows_q[rows, :], (1, 1))
            prob = jnp.exp2(score * (SCALE * LOG2E) - lse)
            seen = jnp.concatenate([pos_s[a] <= q_pos[0], pos_s[a] <= q_pos[1]] * GROUP, axis=1)
            prob = jnp.where(seen, prob, 0.0)
            grad_prob = matmul(val_s[step, a], rows_g[rows, :], (1, 1))
            delta = delta + jnp.sum(prob * grad_prob, axis=0, keepdims=True)
            prob_s[layer, a] = prob
            gp_s[layer, a] = grad_prob
            half_s[a, :, rows] = prob.astype(jnp.bfloat16)
        for a in range(4):
            ds_s[a, :, rows] = (prob_s[layer, a] * (gp_s[layer, a] - delta)).astype(jnp.bfloat16)

    for a, out in enumerate(outs):
        dv = matmul(half_s[a], rows_g[...], (1, 0))
        dk = matmul(ds_s[a], rows_q[...], (1, 0)) * SCALE
        out[:, :, 0] = dk.astype(out.dtype).reshape(4, 4, SLAB, HEAD_DIM)
        out[:, :, 1] = dv.astype(out.dtype).reshape(4, 4, SLAB, HEAD_DIM)

    for layer, (_, _, _, dq_ref) in enumerate(sides):
        rows = slice(layer * WIDE, (layer + 1) * WIDE)
        dq_t = matmul(key_s[step, 0], ds_s[0, :, rows], (0, 0))
        for a in range(1, 4):
            dq_t = dq_t + matmul(key_s[step, a], ds_s[a, :, rows], (0, 0))
        dq_t = dq_t * SCALE
        for h in range(GROUP):
            dq_ref[:, h * 128:(h + 1) * 128] = dq_t[:, h * ROWS:(h + 1) * ROWS].T


def attention(chunk, meta, q_own, g_own, lse_own, q_oth, g_oth, lse_oth, kv, partly):
    def head(g, m):
        return chunk * 4 + m[0] * 2 + g

    q_own, g_own = (pltpu.with_memory_space_constraint(v, pltpu.HBM) for v in (q_own, g_own))
    f32, bf16 = jnp.float32, jnp.bfloat16
    width = GROUP * HEAD_DIM
    own = pl.BlockSpec((ROWS, width), lambda g, m: (0, head(g, m)))
    back = pl.BlockSpec((ROWS, width), lambda g, m: (0, chunk * 2 + g))
    part = pl.BlockSpec((BLOCK, PAYLOAD), lambda g, m: (0, 0))
    lse = pl.BlockSpec((1, 1, WIDE), lambda g, m: (head(g, m), 0, 0))
    out_dims = (4, 4, 2, SLAB, PAIR * HEAD_DIM)
    out = pl.BlockSpec((4, 4, 2, SLAB, HEAD_DIM), lambda g, m: (0, 0, 0, 0, g))
    return pl.pallas_call(
        attention_kernel,
        grid_spec=pltpu.PrefetchScalarGridSpec(
            num_scalar_prefetch=1,
            grid=(PAIR,),
            in_specs=[own, own, lse, own, own, lse, part, part, part, part]
            + [pl.BlockSpec(memory_space=pl.ANY)] * len(partly),
            out_specs=[own, back, out, out, out, out],
            scratch_shapes=[
                pltpu.VMEM((4, BLOCK, 128), f32),
                pltpu.VMEM((PAIR, 4, BLOCK, HEAD_DIM), bf16),
                pltpu.VMEM((PAIR, 4, BLOCK, HEAD_DIM), bf16),
                pltpu.VMEM((2 * WIDE, HEAD_DIM), bf16),
                pltpu.VMEM((2 * WIDE, HEAD_DIM), bf16),
                pltpu.VMEM((2, 4, BLOCK, WIDE), f32),
                pltpu.VMEM((2, 4, BLOCK, WIDE), f32),
                pltpu.VMEM((4, BLOCK, 2 * WIDE), bf16),
                pltpu.VMEM((4, BLOCK, 2 * WIDE), bf16),
            ],
        ),
        out_shape=[
            pltpu.HBM((ROWS, KV_HEADS * width), f32),
            pltpu.HBM((ROWS, KV_HEADS // 2 * width), f32),
            pltpu.HBM(out_dims, f32),
        ] + [pltpu.HBM(out_dims, bf16)] * 3,
        input_output_aliases={11 + n: n for n in range(len(partly))},
        compiler_params=pltpu.CompilerParams(vmem_limit_bytes=36 * 2**20),
        cost_estimate=pl.CostEstimate(
            flops=8 * 10**9, bytes_accessed=8 * 2**20, transcendentals=3 * 10**6
        ),
        name="attention_backward",
    )(meta, q_own, g_own, lse_own, q_oth, g_oth, lse_oth, *kv, *partly)


VMEM = pl.BlockSpec(memory_space=pltpu.VMEM)


def pack_kernel(starts, keys, values, out):
    core, zh, x, y = (lax.axis_index(n) for n in ("core", "zh", "x", "y"))
    offset = starts[0] - (zh * 16 + x * 4 + y) * 256
    tail = jnp.full((SLAB, 128), offset, jnp.int32).astype(jnp.float32).astype(jnp.bfloat16)
    for chunk in range(2):
        cols = pl.ds(pl.multiple_of(chunk * 512 + core * COLS, 128), COLS)
        out[chunk, :, :COLS] = keys[:, cols]
        out[chunk, :, COLS:2 * COLS] = values[:, cols]
        out[chunk, :, 2 * COLS:] = tail


def pack(starts, keys, values):
    keys, values = (pltpu.with_memory_space_constraint(v, pltpu.HBM) for v in (keys, values))
    return pl.pallas_call(
        pack_kernel,
        in_specs=[pl.BlockSpec(memory_space=pltpu.SMEM), VMEM, VMEM],
        out_specs=VMEM,
        out_shape=jax.ShapeDtypeStruct((2, SLAB, PAYLOAD), jnp.bfloat16),
        compiler_params=SMALL,
        name="pack_keys_values",
    )(starts, keys, values)


def line_kernel(own, far, near, next_, out):
    zl, zh = lax.axis_index("zl"), lax.axis_index("zh")
    step = jnp.where(zl == 0, -1, 1)
    for by, block in ((0, own), (2, far), (step, near), (-step, next_)):
        out[:, (zh + by) & 3] = block[...]


def line(blocks):
    return pl.pallas_call(
        line_kernel,
        in_specs=[VMEM] * 4,
        out_specs=VMEM,
        out_shape=jax.ShapeDtypeStruct((2, 4, SLAB, PAYLOAD), jnp.bfloat16),
        compiler_params=SMALL,
        name="join_line",
    )(*blocks)


def plane_place():
    core, x, y = (lax.axis_index(n) for n in ("core", "x", "y"))
    return jnp.where(core == 0, x, y)


def pieces_kernel(*refs):
    b0 = plane_place()
    for r, block in enumerate(refs[:4]):
        for chunk, out in enumerate(refs[4:]):
            out[b0 ^ APART[r]] = block[chunk]


def pieces_of(blocks):
    shape = jax.ShapeDtypeStruct((4, 4, SLAB, PAYLOAD), jnp.bfloat16)
    return pl.pallas_call(
        pieces_kernel,
        in_specs=[VMEM] * 4,
        out_specs=[VMEM, VMEM],
        out_shape=[shape, shape],
        compiler_params=SMALL,
        name="join_pieces",
    )(*blocks)


def share_kernel(*refs):
    b0 = plane_place()
    for r, out in enumerate(refs[-4:]):
        total = refs[0][b0 ^ APART[r]]
        for ref in refs[1:4]:
            total = total + ref[b0 ^ APART[r]].astype(jnp.float32)
        out[0] = total.astype(out.dtype)


def share(chunk, terms, partly):
    dims = terms[0].shape
    whole = pl.BlockSpec(dims, lambda i: (0,) * 5)
    out_dims = (2, *dims[1:])
    return pl.pallas_call(
        share_kernel,
        grid=(1,),
        in_specs=[whole] * 4 + [pl.BlockSpec(memory_space=pl.ANY)] * len(partly),
        out_specs=[pl.BlockSpec((1, *dims[1:]), lambda i: (chunk, 0, 0, 0, 0))] * 4,
        out_shape=[jax.ShapeDtypeStruct(out_dims, jnp.float32)]
        + [jax.ShapeDtypeStruct(out_dims, jnp.bfloat16)] * 3,
        input_output_aliases={4 + n: n for n in range(len(partly))},
        compiler_params=SMALL,
        name="add_first",
    )(*terms, *partly)


def finish_kernel(got, dk, dv):
    for n, out in enumerate((dk, dv)):
        total = got[0, n].astype(jnp.float32)
        for i in range(1, 8):
            total = total + got[i, n].astype(jnp.float32)
        out[...] = total


def finish(got):
    shape = jax.ShapeDtypeStruct((SLAB, 2 * HEAD_DIM), jnp.float32)
    return pl.pallas_call(finish_kernel, out_shape=[shape, shape], compiler_params=SMALL, name="add_last")(got)


def plane_swap(value, by, x_core):
    pairs = []
    for core in range(2):
        for x in range(4):
            for y in range(4):
                to = (x ^ by, y) if core == x_core else (x, y ^ by)
                pairs.append((core * 16 + x * 4 + y, core * 16 + to[0] * 4 + to[1]))
    return lax.ppermute(value, ("core", "x", "y"), pairs)


def plane_swaps(values, x_core):
    return [plane_swap(value, by, x_core) for value, by in zip(values, APART[1:])]


def z_shift(value, by):
    pairs = []
    for z in range(8):
        up = z % 2 == 1
        to = (z + (by if up else -by)) % 8
        pairs.append((z % 2 * 4 + z // 2, to % 2 * 4 + to // 2))
    return lax.ppermute(value, ("zl", "zh"), pairs)


def add(terms):
    total = terms[0].astype(jnp.float32)
    for term in terms[1:]:
        total = total + term.astype(jnp.float32)
    return total.astype(jnp.bfloat16)


def swap(value):
    return lax.ppermute(value, "core", [(0, 1), (1, 0)])


def per_device(
    queries, out_grads, logsumexp, shared_keys, shared_values, query_starts, slab_starts
):
    core, x, y = (lax.axis_index(n) for n in ("core", "x", "y"))
    other = 1 - core
    queries, out_grads, lse = queries[0], out_grads[0], logsumexp[0]

    with jax.named_scope("gather_keys"):
        payload = pack(slab_starts, shared_keys, shared_values)
        block = line([payload] + [z_shift(payload, by) for by in (3, 1, 2)])
        own = pieces_of([block] + plane_swaps([block] * 3, 0))
        pieces = []
        for piece in own:
            piece = piece.reshape(BLOCK, PAYLOAD)
            pieces.append([piece] + plane_swaps([piece] * 3, 1))
    with jax.named_scope("swap_queries"):
        q_oth, g_oth, lse_oth = (swap(v) for v in (queries, out_grads, lse))

    a0 = jnp.where(core == 0, y, x)
    meta = jnp.stack([core, a0, query_starts[0]]).astype(jnp.int32)
    wide = (KV_HEADS, 1, WIDE)
    lse, lse_oth = lse.reshape(wide), lse_oth.reshape(wide)
    partly, sums = [], []
    for chunk in range(2):
        *partly, part0, part1, part2, part3 = attention(
            chunk, meta, queries, out_grads, lse, q_oth, g_oth, lse_oth, pieces[chunk], partly
        )
        with jax.named_scope("scatter_grads"):
            if sums:
                part0, part1, part2, part3, partly, sums = lax.optimization_barrier(
                    (part0, part1, part2, part3, partly, sums)
                )
            sums.append([part0, *plane_swaps([part1, part2, part3], 1)])

    dq, dq_oth = partly
    with jax.named_scope("scatter_grads"):
        mine, *shares = share(1, sums[1], share(0, sums[0], []))
        shares = plane_swaps(shares, 0)
    with jax.named_scope("swap_query_grads"):
        dq_oth, _ = lax.optimization_barrier((dq_oth, mine))
        back = swap(dq_oth)
        dq = lax.dynamic_update_slice(dq, back[:, :768], (0, other * 768))
        dq = lax.dynamic_update_slice(dq, back[:, 768:], (0, (2 + other) * 768))
    with jax.named_scope("scatter_grads"):
        shares[0], dq = lax.optimization_barrier((shares[0], dq))
        small = add([mine, *shares]).reshape(8, 2, SLAB, 2 * HEAD_DIM)
        dk, dv = finish(lax.all_to_all(small, ("zl", "zh"), 0, 0))
    return dq[None], dk, dv


def solution(mesh):
    fine = Mesh(mesh.devices.reshape(2, 2, 4, 4, 4), AXES)
    section, seq = ("zl", "core"), ("zh", "x", "y")
    return jax.shard_map(
        per_device,
        mesh=fine,
        in_specs=(
            P(section, seq, None),
            P(section, seq, None),
            P(section, None, seq),
            P(seq, None),
            P(seq, None),
            P(seq),
            P(seq),
        ),
        out_specs=(P(section, seq, None), P(seq, section), P(seq, section)),
        check_vma=False,
    )
```

```python
import jax
import jax.numpy as jnp
from jax import lax
from jax.experimental import pallas as pl
from jax.experimental.pallas import tpu as pltpu
from jax.sharding import Mesh
from jax.sharding import PartitionSpec as P

KV_HEADS = 8
GROUP = 3
HEAD_DIM = 128
ROWS = 256
SLAB = 16
SCALE = HEAD_DIM**-0.5
LOG2E = 1.4426950408889634
WIDE = GROUP * ROWS
PAIR = 2
COLS = PAIR * HEAD_DIM
PAYLOAD = 2 * COLS + 128
BLOCK = 256
KEYS = 4 * BLOCK
APART = (0, 2, 1, 3)
AXES = ("zl", "core", "zh", "x", "y")


SMALL = pltpu.CompilerParams(vmem_limit_bytes=8 * 2**20)


def matmul(left, right, contract):
    return lax.dot_general(
        left, right, ((contract[:1], contract[1:]), ((), ())), preferred_element_type=jnp.float32
    )


def attention_kernel(
    meta, q_own, g_own, lse_own, q_oth, g_oth, lse_oth, kv0, kv1, kv2, kv3, *rest
):
    (
        dq_own, dq_oth, out0, out1, out2, out3,
        pos_s, key_s, val_s, rows_q, rows_g, prob_s, gp_s, half_s, ds_s,
    ) = rest[-15:]
    step = pl.program_id(0)
    core, a0, first = (meta[i] for i in range(3))
    pieces = (kv0, kv1, kv2, kv3)
    outs = (out0, out1, out2, out3)

    @pl.when(step == 0)
    def _():
        a_step = jnp.where(core == 0, 1, 4)
        b_step = jnp.where(core == 0, 4, 1)
        row = lax.broadcasted_iota(jnp.int32, (BLOCK, 128), 0)
        base = (((row >> 4) & 3) * 16 + (row >> 6) * b_step) * 256 + (row & 15)
        for a, piece in enumerate(pieces):
            slab = (a0 ^ APART[a]) * a_step
            sl = slice(a * BLOCK, (a + 1) * BLOCK)
            offset = piece[BLOCK:, :128].astype(jnp.float32).reshape(SLAB, 1, 128)
            offset = jnp.broadcast_to(offset, (SLAB, SLAB, 128)).reshape(BLOCK, 128)
            pos_s[sl, :] = offset + (base + slab * 256).astype(jnp.float32)
            for h in range(PAIR):
                key_s[h, sl, :] = piece[:BLOCK, h * 128:(h + 1) * 128]
                val_s[h, sl, :] = piece[:BLOCK, COLS + h * 128:COLS + (h + 1) * 128]

    lane = lax.broadcasted_iota(jnp.int32, (1, 128), 1)
    q_pos = [(first + lane + c * 128).astype(jnp.float32) for c in range(2)]
    sides = ((q_own, g_own, lse_own, dq_own), (q_oth, g_oth, lse_oth, dq_oth))

    for layer, (q_ref, g_ref, _, _) in enumerate(sides):
        for h in range(GROUP):
            rows = slice(layer * WIDE + h * ROWS, layer * WIDE + (h + 1) * ROWS)
            rows_q[rows, :] = q_ref[:, h * 128:(h + 1) * 128]
            rows_g[rows, :] = g_ref[:, h * 128:(h + 1) * 128]

    for layer, (_, _, lse_ref, _) in enumerate(sides):
        rows = slice(layer * WIDE, (layer + 1) * WIDE)
        lse = lse_ref[0] * LOG2E
        delta = jnp.zeros((1, WIDE), jnp.float32)
        for low in range(0, KEYS, BLOCK):
            sl = slice(low, low + BLOCK)
            score = matmul(key_s[step, sl, :], rows_q[rows, :], (1, 1))
            prob = jnp.exp2(score * (SCALE * LOG2E) - lse)
            seen = jnp.concatenate([pos_s[sl, :] <= q_pos[0], pos_s[sl, :] <= q_pos[1]] * GROUP, axis=1)
            prob = jnp.where(seen, prob, 0.0)
            grad_prob = matmul(val_s[step, sl, :], rows_g[rows, :], (1, 1))
            delta = delta + jnp.sum(prob * grad_prob, axis=0, keepdims=True)
            prob_s[layer, sl, :] = prob
            gp_s[layer, sl, :] = grad_prob
            half_s[sl, rows] = prob.astype(jnp.bfloat16)
        for low in range(0, KEYS, BLOCK):
            sl = slice(low, low + BLOCK)
            ds_s[sl, rows] = (prob_s[layer, sl, :] * (gp_s[layer, sl, :] - delta)).astype(jnp.bfloat16)

    dv = matmul(half_s[...], rows_g[...], (1, 0))
    dk = matmul(ds_s[...], rows_q[...], (1, 0)) * SCALE
    for a, out in enumerate(outs):
        sl = slice(a * BLOCK, (a + 1) * BLOCK)
        out[:, :, 0] = dk[sl].astype(out.dtype).reshape(4, 4, SLAB, HEAD_DIM)
        out[:, :, 1] = dv[sl].astype(out.dtype).reshape(4, 4, SLAB, HEAD_DIM)

    for layer, (_, _, _, dq_ref) in enumerate(sides):
        rows = slice(layer * WIDE, (layer + 1) * WIDE)
        dq_t = matmul(key_s[step], ds_s[:, rows], (0, 0)) * SCALE
        for h in range(GROUP):
            dq_ref[:, h * 128:(h + 1) * 128] = dq_t[:, h * ROWS:(h + 1) * ROWS].T


def attention(chunk, meta, q_own, g_own, lse_own, q_oth, g_oth, lse_oth, kv, partly):
    def head(g, m):
        return chunk * 4 + m[0] * 2 + g

    q_own, g_own = (pltpu.with_memory_space_constraint(v, pltpu.HBM) for v in (q_own, g_own))
    f32, bf16 = jnp.float32, jnp.bfloat16
    width = GROUP * HEAD_DIM
    own = pl.BlockSpec((ROWS, width), lambda g, m: (0, head(g, m)))
    back = pl.BlockSpec((ROWS, width), lambda g, m: (0, chunk * 2 + g))
    part = pl.BlockSpec(kv[0].shape, lambda g, m: (0, 0))
    lse = pl.BlockSpec((1, 1, WIDE), lambda g, m: (head(g, m), 0, 0))
    out_dims = (4, 4, 2, SLAB, PAIR * HEAD_DIM)
    out = pl.BlockSpec((4, 4, 2, SLAB, HEAD_DIM), lambda g, m: (0, 0, 0, 0, g))
    return pl.pallas_call(
        attention_kernel,
        grid_spec=pltpu.PrefetchScalarGridSpec(
            num_scalar_prefetch=1,
            grid=(PAIR,),
            in_specs=[own, own, lse, own, own, lse, part, part, part, part]
            + [pl.BlockSpec(memory_space=pl.ANY)] * len(partly),
            out_specs=[own, back, out, out, out, out],
            scratch_shapes=[
                pltpu.VMEM((KEYS, 128), f32),
                pltpu.VMEM((PAIR, KEYS, HEAD_DIM), bf16),
                pltpu.VMEM((PAIR, KEYS, HEAD_DIM), bf16),
                pltpu.VMEM((2 * WIDE, HEAD_DIM), bf16),
                pltpu.VMEM((2 * WIDE, HEAD_DIM), bf16),
                pltpu.VMEM((2, KEYS, WIDE), f32),
                pltpu.VMEM((2, KEYS, WIDE), f32),
                pltpu.VMEM((KEYS, 2 * WIDE), bf16),
                pltpu.VMEM((KEYS, 2 * WIDE), bf16),
            ],
        ),
        out_shape=[
            pltpu.HBM((ROWS, KV_HEADS * width), f32),
            pltpu.HBM((ROWS, KV_HEADS // 2 * width), f32),
            pltpu.HBM(out_dims, f32),
        ] + [pltpu.HBM(out_dims, bf16)] * 3,
        input_output_aliases={11 + n: n for n in range(len(partly))},
        compiler_params=pltpu.CompilerParams(vmem_limit_bytes=36 * 2**20),
        cost_estimate=pl.CostEstimate(
            flops=8 * 10**9, bytes_accessed=8 * 2**20, transcendentals=3 * 10**6
        ),
        name="attention_backward",
    )(meta, q_own, g_own, lse_own, q_oth, g_oth, lse_oth, *kv, *partly)


VMEM = pl.BlockSpec(memory_space=pltpu.VMEM)


def pack_kernel(starts, keys, values, out):
    core, zh, x, y = (lax.axis_index(n) for n in ("core", "zh", "x", "y"))
    offset = starts[0] - (zh * 16 + x * 4 + y) * 256
    tail = jnp.full((SLAB, 128), offset, jnp.int32).astype(jnp.float32).astype(jnp.bfloat16)
    for chunk in range(2):
        cols = pl.ds(pl.multiple_of(chunk * 512 + core * COLS, 128), COLS)
        out[chunk, :, :COLS] = keys[:, cols]
        out[chunk, :, COLS:2 * COLS] = values[:, cols]
        out[chunk, :, 2 * COLS:] = tail


def pack(starts, keys, values):
    keys, values = (pltpu.with_memory_space_constraint(v, pltpu.HBM) for v in (keys, values))
    return pl.pallas_call(
        pack_kernel,
        in_specs=[pl.BlockSpec(memory_space=pltpu.SMEM), VMEM, VMEM],
        out_specs=VMEM,
        out_shape=jax.ShapeDtypeStruct((2, SLAB, PAYLOAD), jnp.bfloat16),
        compiler_params=SMALL,
        name="pack_keys_values",
    )(starts, keys, values)


def line_kernel(own, far, near, next_, out):
    zl, zh = lax.axis_index("zl"), lax.axis_index("zh")
    step = jnp.where(zl == 0, -1, 1)
    for by, block in ((0, own), (2, far), (step, near), (-step, next_)):
        out[:, (zh + by) & 3] = block[...]


def line(blocks):
    return pl.pallas_call(
        line_kernel,
        in_specs=[VMEM] * 4,
        out_specs=VMEM,
        out_shape=jax.ShapeDtypeStruct((2, 4, SLAB, PAYLOAD), jnp.bfloat16),
        compiler_params=SMALL,
        name="join_line",
    )(*blocks)


def plane_place():
    core, x, y = (lax.axis_index(n) for n in ("core", "x", "y"))
    return jnp.where(core == 0, x, y)


def pieces_kernel(*refs):
    b0 = plane_place()
    row = lax.broadcasted_iota(jnp.int32, (SLAB, 128), 0)
    for chunk, out in enumerate(refs[4:]):
        tail = jnp.zeros((SLAB, 128), jnp.float32)
        for r, block in enumerate(refs[:4]):
            for z in range(4):
                place = (b0 ^ APART[r]) * 4 + z
                out[place] = block[chunk, z, :, :2 * COLS]
                offset = block[chunk, z, :, 2 * COLS:].astype(jnp.float32)
                tail = jnp.where(row == place, offset, tail)
        out[SLAB] = jnp.concatenate([tail] * (2 * COLS // 128), 1).astype(jnp.bfloat16)


def pieces_of(blocks):
    shape = jax.ShapeDtypeStruct((SLAB + 1, SLAB, 2 * COLS), jnp.bfloat16)
    return pl.pallas_call(
        pieces_kernel,
        in_specs=[VMEM] * 4,
        out_specs=[VMEM, VMEM],
        out_shape=[shape, shape],
        compiler_params=SMALL,
        name="join_pieces",
    )(*blocks)


def share_kernel(*refs):
    b0 = plane_place()
    for r, out in enumerate(refs[-4:]):
        total = refs[0][b0 ^ APART[r]]
        for ref in refs[1:4]:
            total = total + ref[b0 ^ APART[r]].astype(jnp.float32)
        out[0] = total.astype(out.dtype)


def share(chunk, terms, partly):
    dims = terms[0].shape
    whole = pl.BlockSpec(dims, lambda i: (0,) * 5)
    out_dims = (2, *dims[1:])
    return pl.pallas_call(
        share_kernel,
        grid=(1,),
        in_specs=[whole] * 4 + [pl.BlockSpec(memory_space=pl.ANY)] * len(partly),
        out_specs=[pl.BlockSpec((1, *dims[1:]), lambda i: (chunk, 0, 0, 0, 0))] * 4,
        out_shape=[jax.ShapeDtypeStruct(out_dims, jnp.float32)]
        + [jax.ShapeDtypeStruct(out_dims, jnp.bfloat16)] * 3,
        input_output_aliases={4 + n: n for n in range(len(partly))},
        compiler_params=SMALL,
        name="add_first",
    )(*terms, *partly)


def finish_kernel(got, dk, dv):
    for n, out in enumerate((dk, dv)):
        total = got[0, n].astype(jnp.float32)
        for i in range(1, 8):
            total = total + got[i, n].astype(jnp.float32)
        out[...] = total


def finish(got):
    shape = jax.ShapeDtypeStruct((SLAB, 2 * HEAD_DIM), jnp.float32)
    return pl.pallas_call(finish_kernel, out_shape=[shape, shape], compiler_params=SMALL, name="add_last")(got)


def plane_swap(value, by, x_core):
    pairs = []
    for core in range(2):
        for x in range(4):
            for y in range(4):
                to = (x ^ by, y) if core == x_core else (x, y ^ by)
                pairs.append((core * 16 + x * 4 + y, core * 16 + to[0] * 4 + to[1]))
    return lax.ppermute(value, ("core", "x", "y"), pairs)


def plane_swaps(values, x_core):
    return [plane_swap(value, by, x_core) for value, by in zip(values, APART[1:])]


def z_shift(value, by):
    pairs = []
    for z in range(8):
        up = z % 2 == 1
        to = (z + (by if up else -by)) % 8
        pairs.append((z % 2 * 4 + z // 2, to % 2 * 4 + to // 2))
    return lax.ppermute(value, ("zl", "zh"), pairs)


def add(terms):
    total = terms[0].astype(jnp.float32)
    for term in terms[1:]:
        total = total + term.astype(jnp.float32)
    return total.astype(jnp.bfloat16)


def swap(value):
    return lax.ppermute(value, "core", [(0, 1), (1, 0)])


def per_device(
    queries, out_grads, logsumexp, shared_keys, shared_values, query_starts, slab_starts
):
    core, x, y = (lax.axis_index(n) for n in ("core", "x", "y"))
    other = 1 - core
    queries, out_grads, lse = queries[0], out_grads[0], logsumexp[0]

    with jax.named_scope("gather_keys"):
        payload = pack(slab_starts, shared_keys, shared_values)
        q_sent, g_sent, payload = lax.optimization_barrier((queries, out_grads, payload))
        block = line([payload] + [z_shift(payload, by) for by in (3, 1, 2)])
        with jax.named_scope("swap_queries"):
            q_oth, g_oth, lse_oth = (swap(v) for v in (q_sent, g_sent, lse))
        own = pieces_of([block] + plane_swaps([block] * 3, 0))
        pieces = []
        for piece in own:
            piece = piece.reshape(BLOCK + SLAB, 2 * COLS)
            pieces.append([piece] + plane_swaps([piece] * 3, 1))
    a0 = jnp.where(core == 0, y, x)
    meta = jnp.stack([core, a0, query_starts[0]]).astype(jnp.int32)
    wide = (KV_HEADS, 1, WIDE)
    lse, lse_oth = lse.reshape(wide), lse_oth.reshape(wide)
    partly, sums = [], []
    for chunk in range(2):
        *partly, part0, part1, part2, part3 = attention(
            chunk, meta, queries, out_grads, lse, q_oth, g_oth, lse_oth, pieces[chunk], partly
        )
        with jax.named_scope("scatter_grads"):
            if sums:
                part0, part1, part2, part3, partly, sums = lax.optimization_barrier(
                    (part0, part1, part2, part3, partly, sums)
                )
            sums.append([part0, *plane_swaps([part1, part2, part3], 1)])

    dq, dq_oth = partly
    with jax.named_scope("scatter_grads"):
        first_shares = share(0, sums[0], [])
    with jax.named_scope("swap_query_grads"):
        dq_oth, first_shares = lax.optimization_barrier((dq_oth, first_shares))
        back = swap(dq_oth)
        dq = lax.dynamic_update_slice(dq, back[:, :768], (0, other * 768))
        dq = lax.dynamic_update_slice(dq, back[:, 768:], (0, (2 + other) * 768))
    with jax.named_scope("scatter_grads"):
        mine, *shares = share(1, sums[1], first_shares)
        shares = plane_swaps(shares, 0)
        shares[0], dq = lax.optimization_barrier((shares[0], dq))
        small = add([mine, *shares]).reshape(8, 2, SLAB, 2 * HEAD_DIM)
        dk, dv = finish(lax.all_to_all(small, ("zl", "zh"), 0, 0))
    return dq[None], dk, dv


def solution(mesh):
    fine = Mesh(mesh.devices.reshape(2, 2, 4, 4, 4), AXES)
    section, seq = ("zl", "core"), ("zh", "x", "y")
    return jax.shard_map(
        per_device,
        mesh=fine,
        in_specs=(
            P(section, seq, None),
            P(section, seq, None),
            P(section, None, seq),
            P(seq, None),
            P(seq, None),
            P(seq),
            P(seq),
        ),
        out_specs=(P(section, seq, None), P(seq, section), P(seq, section)),
        check_vma=False,
    )
```

```python
import jax
import jax.numpy as jnp
from jax import lax
from jax.experimental import pallas as pl
from jax.experimental.pallas import tpu as pltpu
from jax.sharding import Mesh
from jax.sharding import PartitionSpec as P

KV_HEADS = 8
GROUP = 3
HEAD_DIM = 128
ROWS = 256
SLAB = 16
SCALE = HEAD_DIM**-0.5
LOG2E = 1.4426950408889634
WIDE = GROUP * ROWS
PAIR = 2
COLS = PAIR * HEAD_DIM
PAYLOAD = 2 * COLS + 128
BLOCK = 256
KEYS = 4 * BLOCK
APART = (0, 2, 1, 3)
AXES = ("zl", "core", "zh", "x", "y")


SMALL = pltpu.CompilerParams(vmem_limit_bytes=8 * 2**20)


def matmul(left, right, contract):
    return lax.dot_general(
        left, right, ((contract[:1], contract[1:]), ((), ())), preferred_element_type=jnp.float32
    )


def attention_kernel(
    meta, q_own, g_own, lse_own, q_oth, g_oth, lse_oth, kv0, kv1, kv2, kv3, *rest
):
    (
        dq_own, dq_oth, out0, out1, out2, out3,
        pos_s, key_s, val_s, rows_q, rows_g, prob_s, gp_s, half_s, ds_s,
    ) = rest[-15:]
    step = pl.program_id(0)
    core, a0, first = (meta[i] for i in range(3))
    pieces = (kv0, kv1, kv2, kv3)
    outs = (out0, out1, out2, out3)

    @pl.when(step == 0)
    def _():
        a_step = jnp.where(core == 0, 1, 4)
        b_step = jnp.where(core == 0, 4, 1)
        row = lax.broadcasted_iota(jnp.int32, (BLOCK, 128), 0)
        base = (((row >> 4) & 3) * 16 + (row >> 6) * b_step) * 256 + (row & 15)
        for a, piece in enumerate(pieces):
            slab = (a0 ^ APART[a]) * a_step
            sl = slice(a * BLOCK, (a + 1) * BLOCK)
            offset = piece[BLOCK:, :128].astype(jnp.float32).reshape(SLAB, 1, 128)
            offset = jnp.broadcast_to(offset, (SLAB, SLAB, 128)).reshape(BLOCK, 128)
            pos_s[sl, :] = offset + (base + slab * 256).astype(jnp.float32)
            for h in range(PAIR):
                key_s[h, sl, :] = piece[:BLOCK, h * 128:(h + 1) * 128]
                val_s[h, sl, :] = piece[:BLOCK, COLS + h * 128:COLS + (h + 1) * 128]

    lane = lax.broadcasted_iota(jnp.int32, (1, 128), 1)
    q_pos = [(first + lane + c * 128).astype(jnp.float32) for c in range(2)]
    sides = ((q_own, g_own, lse_own, dq_own), (q_oth, g_oth, lse_oth, dq_oth))

    for layer, (q_ref, g_ref, _, _) in enumerate(sides):
        for h in range(GROUP):
            rows = slice(layer * WIDE + h * ROWS, layer * WIDE + (h + 1) * ROWS)
            rows_q[rows, :] = q_ref[:, h * 128:(h + 1) * 128]
            rows_g[rows, :] = g_ref[:, h * 128:(h + 1) * 128]

    for layer, (_, _, lse_ref, _) in enumerate(sides):
        rows = slice(layer * WIDE, (layer + 1) * WIDE)
        lse = lse_ref[0] * LOG2E
        delta = jnp.zeros((1, WIDE), jnp.float32)
        for low in range(0, KEYS, BLOCK):
            sl = slice(low, low + BLOCK)
            score = matmul(key_s[step, sl, :], rows_q[rows, :], (1, 1))
            prob = jnp.exp2(score * (SCALE * LOG2E) - lse)
            seen = jnp.concatenate([pos_s[sl, :] <= q_pos[0], pos_s[sl, :] <= q_pos[1]] * GROUP, axis=1)
            prob = jnp.where(seen, prob, 0.0)
            grad_prob = matmul(val_s[step, sl, :], rows_g[rows, :], (1, 1))
            delta = delta + jnp.sum(prob * grad_prob, axis=0, keepdims=True)
            prob_s[layer, sl, :] = prob
            gp_s[layer, sl, :] = grad_prob
            half_s[sl, rows] = prob.astype(jnp.bfloat16)
        for low in range(0, KEYS, BLOCK):
            sl = slice(low, low + BLOCK)
            ds_s[sl, rows] = (prob_s[layer, sl, :] * (gp_s[layer, sl, :] - delta)).astype(jnp.bfloat16)

    dv = matmul(half_s[...], rows_g[...], (1, 0))
    dk = matmul(ds_s[...], rows_q[...], (1, 0)) * SCALE
    for a, out in enumerate(outs):
        sl = slice(a * BLOCK, (a + 1) * BLOCK)
        out[:, :, 0] = dk[sl].astype(out.dtype).reshape(4, 4, SLAB, HEAD_DIM)
        out[:, :, 1] = dv[sl].astype(out.dtype).reshape(4, 4, SLAB, HEAD_DIM)

    for layer, (_, _, _, dq_ref) in enumerate(sides):
        rows = slice(layer * WIDE, (layer + 1) * WIDE)
        dq_t = matmul(key_s[step], ds_s[:, rows], (0, 0)) * SCALE
        for h in range(GROUP):
            dq_ref[:, h * 128:(h + 1) * 128] = dq_t[:, h * ROWS:(h + 1) * ROWS].T


def attention(chunk, meta, q_own, g_own, lse_own, q_oth, g_oth, lse_oth, kv, partly):
    def head(g, m):
        return chunk * 4 + m[0] * 2 + g

    q_own, g_own = (pltpu.with_memory_space_constraint(v, pltpu.HBM) for v in (q_own, g_own))
    f32, bf16 = jnp.float32, jnp.bfloat16
    width = GROUP * HEAD_DIM
    own = pl.BlockSpec((ROWS, width), lambda g, m: (0, head(g, m)))
    back = pl.BlockSpec((ROWS, width), lambda g, m: (0, chunk * 2 + g))
    part = pl.BlockSpec(kv[0].shape, lambda g, m: (0, 0))
    lse = pl.BlockSpec((1, 1, WIDE), lambda g, m: (head(g, m), 0, 0))
    out_dims = (4, 4, 2, SLAB, PAIR * HEAD_DIM)
    out = pl.BlockSpec((4, 4, 2, SLAB, HEAD_DIM), lambda g, m: (0, 0, 0, 0, g))
    return pl.pallas_call(
        attention_kernel,
        grid_spec=pltpu.PrefetchScalarGridSpec(
            num_scalar_prefetch=1,
            grid=(PAIR,),
            in_specs=[own, own, lse, own, own, lse, part, part, part, part]
            + [pl.BlockSpec(memory_space=pl.ANY)] * len(partly),
            out_specs=[own, back, out, out, out, out],
            scratch_shapes=[
                pltpu.VMEM((KEYS, 128), f32),
                pltpu.VMEM((PAIR, KEYS, HEAD_DIM), bf16),
                pltpu.VMEM((PAIR, KEYS, HEAD_DIM), bf16),
                pltpu.VMEM((2 * WIDE, HEAD_DIM), bf16),
                pltpu.VMEM((2 * WIDE, HEAD_DIM), bf16),
                pltpu.VMEM((2, KEYS, WIDE), f32),
                pltpu.VMEM((2, KEYS, WIDE), f32),
                pltpu.VMEM((KEYS, 2 * WIDE), bf16),
                pltpu.VMEM((KEYS, 2 * WIDE), bf16),
            ],
        ),
        out_shape=[
            pltpu.HBM((ROWS, KV_HEADS * width), f32),
            pltpu.HBM((ROWS, KV_HEADS // 2 * width), f32),
            pltpu.HBM(out_dims, f32),
        ] + [pltpu.HBM(out_dims, bf16)] * 3,
        input_output_aliases={11 + n: n for n in range(len(partly))},
        compiler_params=pltpu.CompilerParams(vmem_limit_bytes=36 * 2**20),
        cost_estimate=pl.CostEstimate(
            flops=8 * 10**9, bytes_accessed=8 * 2**20, transcendentals=3 * 10**6
        ),
        name="attention_backward",
    )(meta, q_own, g_own, lse_own, q_oth, g_oth, lse_oth, *kv, *partly)


VMEM = pl.BlockSpec(memory_space=pltpu.VMEM)


def pack_kernel(starts, keys, values, out):
    core, zh, x, y = (lax.axis_index(n) for n in ("core", "zh", "x", "y"))
    offset = starts[0] - (zh * 16 + x * 4 + y) * 256
    tail = jnp.full((SLAB, 128), offset, jnp.int32).astype(jnp.float32).astype(jnp.bfloat16)
    for chunk in range(2):
        cols = pl.ds(pl.multiple_of(chunk * 512 + core * COLS, 128), COLS)
        out[chunk, :, :COLS] = keys[:, cols]
        out[chunk, :, COLS:2 * COLS] = values[:, cols]
        out[chunk, :, 2 * COLS:] = tail


def pack(starts, keys, values):
    keys, values = (pltpu.with_memory_space_constraint(v, pltpu.HBM) for v in (keys, values))
    return pl.pallas_call(
        pack_kernel,
        in_specs=[pl.BlockSpec(memory_space=pltpu.SMEM), VMEM, VMEM],
        out_specs=VMEM,
        out_shape=jax.ShapeDtypeStruct((2, SLAB, PAYLOAD), jnp.bfloat16),
        compiler_params=SMALL,
        name="pack_keys_values",
    )(starts, keys, values)


def line_kernel(own, far, near, next_, out):
    zl, zh = lax.axis_index("zl"), lax.axis_index("zh")
    step = jnp.where(zl == 0, -1, 1)
    for by, block in ((0, own), (2, far), (step, near), (-step, next_)):
        out[:, (zh + by) & 3] = block[...]


def line(blocks):
    return pl.pallas_call(
        line_kernel,
        in_specs=[VMEM] * 4,
        out_specs=VMEM,
        out_shape=jax.ShapeDtypeStruct((2, 4, SLAB, PAYLOAD), jnp.bfloat16),
        compiler_params=SMALL,
        name="join_line",
    )(*blocks)


def plane_place():
    core, x, y = (lax.axis_index(n) for n in ("core", "x", "y"))
    return jnp.where(core == 0, x, y)


def pieces_kernel(*refs):
    b0 = plane_place()
    row = lax.broadcasted_iota(jnp.int32, (SLAB, 128), 0)
    for chunk, out in enumerate(refs[4:]):
        tail = jnp.zeros((SLAB, 128), jnp.float32)
        for r, block in enumerate(refs[:4]):
            for z in range(4):
                place = (b0 ^ APART[r]) * 4 + z
                out[place] = block[chunk, z, :, :2 * COLS]
                offset = block[chunk, z, :, 2 * COLS:].astype(jnp.float32)
                tail = jnp.where(row == place, offset, tail)
        out[SLAB] = jnp.concatenate([tail] * (2 * COLS // 128), 1).astype(jnp.bfloat16)


def pieces_of(blocks):
    shape = jax.ShapeDtypeStruct((SLAB + 1, SLAB, 2 * COLS), jnp.bfloat16)
    return pl.pallas_call(
        pieces_kernel,
        in_specs=[VMEM] * 4,
        out_specs=[VMEM, VMEM],
        out_shape=[shape, shape],
        compiler_params=SMALL,
        name="join_pieces",
    )(*blocks)


def share_kernel(*refs):
    b0 = plane_place()
    for r, out in enumerate(refs[-4:]):
        total = refs[0][b0 ^ APART[r]]
        for ref in refs[1:4]:
            total = total + ref[b0 ^ APART[r]].astype(jnp.float32)
        out[0] = total.astype(out.dtype)


def share(chunk, terms, partly):
    dims = terms[0].shape
    whole = pl.BlockSpec(dims, lambda i: (0,) * 5)
    out_dims = (2, *dims[1:])
    return pl.pallas_call(
        share_kernel,
        grid=(1,),
        in_specs=[whole] * 4 + [pl.BlockSpec(memory_space=pl.ANY)] * len(partly),
        out_specs=[pl.BlockSpec((1, *dims[1:]), lambda i: (chunk, 0, 0, 0, 0))] * 4,
        out_shape=[jax.ShapeDtypeStruct(out_dims, jnp.float32)]
        + [jax.ShapeDtypeStruct(out_dims, jnp.bfloat16)] * 3,
        input_output_aliases={4 + n: n for n in range(len(partly))},
        compiler_params=SMALL,
        name="add_first",
    )(*terms, *partly)


def finish_kernel(got, dk, dv):
    for n, out in enumerate((dk, dv)):
        total = got[0, n].astype(jnp.float32)
        for i in range(1, 8):
            total = total + got[i, n].astype(jnp.float32)
        out[...] = total


def finish(got):
    shape = jax.ShapeDtypeStruct((SLAB, 2 * HEAD_DIM), jnp.float32)
    return pl.pallas_call(finish_kernel, out_shape=[shape, shape], compiler_params=SMALL, name="add_last")(got)


def plane_swap(value, by, x_core):
    pairs = []
    for core in range(2):
        for x in range(4):
            for y in range(4):
                to = (x ^ by, y) if core == x_core else (x, y ^ by)
                pairs.append((core * 16 + x * 4 + y, core * 16 + to[0] * 4 + to[1]))
    return lax.ppermute(value, ("core", "x", "y"), pairs)


def plane_swaps(values, x_core):
    return [plane_swap(value, by, x_core) for value, by in zip(values, APART[1:])]


def z_shift(value, by):
    pairs = []
    for z in range(8):
        up = z % 2 == 1
        to = (z + (by if up else -by)) % 8
        pairs.append((z % 2 * 4 + z // 2, to % 2 * 4 + to // 2))
    return lax.ppermute(value, ("zl", "zh"), pairs)


def add(terms):
    total = terms[0].astype(jnp.float32)
    for term in terms[1:]:
        total = total + term.astype(jnp.float32)
    return total.astype(jnp.bfloat16)


def swap(value):
    return lax.ppermute(value, "core", [(0, 1), (1, 0)])


def per_device(
    queries, out_grads, logsumexp, shared_keys, shared_values, query_starts, slab_starts
):
    core, x, y = (lax.axis_index(n) for n in ("core", "x", "y"))
    other = 1 - core
    queries, out_grads, lse = queries[0], out_grads[0], logsumexp[0]

    with jax.named_scope("gather_keys"):
        payload = pack(slab_starts, shared_keys, shared_values)
        q_sent, g_sent, payload = lax.optimization_barrier((queries, out_grads, payload))
        block = line([payload] + [z_shift(payload, by) for by in (3, 1, 2)])
        with jax.named_scope("swap_queries"):
            q_oth, g_oth, lse_oth = (swap(v) for v in (q_sent, g_sent, lse))
        blocks = [block] + plane_swaps([block] * 3, 0)
        blocks, q_oth, g_oth = lax.optimization_barrier((blocks, q_oth, g_oth))
        own = pieces_of(blocks)
        pieces = []
        for piece in own:
            piece = piece.reshape(BLOCK + SLAB, 2 * COLS)
            pieces.append([piece] + plane_swaps([piece] * 3, 1))
    a0 = jnp.where(core == 0, y, x)
    meta = jnp.stack([core, a0, query_starts[0]]).astype(jnp.int32)
    wide = (KV_HEADS, 1, WIDE)
    lse, lse_oth = lse.reshape(wide), lse_oth.reshape(wide)
    partly, sums = [], []
    for chunk in range(2):
        *partly, part0, part1, part2, part3 = attention(
            chunk, meta, queries, out_grads, lse, q_oth, g_oth, lse_oth, pieces[chunk], partly
        )
        with jax.named_scope("scatter_grads"):
            if sums:
                part0, part1, part2, part3, partly, sums = lax.optimization_barrier(
                    (part0, part1, part2, part3, partly, sums)
                )
            sums.append([part0, *plane_swaps([part1, part2, part3], 1)])

    dq, dq_oth = partly
    with jax.named_scope("scatter_grads"):
        first_shares = share(0, sums[0], [])
    with jax.named_scope("swap_query_grads"):
        dq_oth, first_shares = lax.optimization_barrier((dq_oth, first_shares))
        back = swap(dq_oth)
        dq = lax.dynamic_update_slice(dq, back[:, :768], (0, other * 768))
        dq = lax.dynamic_update_slice(dq, back[:, 768:], (0, (2 + other) * 768))
    with jax.named_scope("scatter_grads"):
        mine, *shares = share(1, sums[1], first_shares)
        shares = plane_swaps(shares, 0)
        shares[0], dq = lax.optimization_barrier((shares[0], dq))
        small = add([mine, *shares]).reshape(8, 2, SLAB, 2 * HEAD_DIM)
        dk, dv = finish(lax.all_to_all(small, ("zl", "zh"), 0, 0))
    return dq[None], dk, dv


def solution(mesh):
    fine = Mesh(mesh.devices.reshape(2, 2, 4, 4, 4), AXES)
    section, seq = ("zl", "core"), ("zh", "x", "y")
    return jax.shard_map(
        per_device,
        mesh=fine,
        in_specs=(
            P(section, seq, None),
            P(section, seq, None),
            P(section, None, seq),
            P(seq, None),
            P(seq, None),
            P(seq),
            P(seq),
        ),
        out_specs=(P(section, seq, None), P(seq, section), P(seq, section)),
        check_vma=False,
    )
```

```python
import jax
import jax.numpy as jnp
from jax import lax
from jax.experimental import pallas as pl
from jax.experimental.pallas import tpu as pltpu
from jax.sharding import Mesh
from jax.sharding import PartitionSpec as P

KV_HEADS = 8
GROUP = 3
HEAD_DIM = 128
ROWS = 256
SLAB = 16
SCALE = HEAD_DIM**-0.5
LOG2E = 1.4426950408889634
WIDE = GROUP * ROWS
PAIR = 2
COLS = PAIR * HEAD_DIM
PAYLOAD = 2 * COLS + 128
BLOCK = 256
KEYS = 4 * BLOCK
APART = (0, 2, 1, 3)
AXES = ("zl", "core", "zh", "x", "y")


SMALL = pltpu.CompilerParams(vmem_limit_bytes=8 * 2**20)


def matmul(left, right, contract):
    return lax.dot_general(
        left, right, ((contract[:1], contract[1:]), ((), ())), preferred_element_type=jnp.float32
    )


def attention_kernel(
    meta, q_own, g_own, lse_own, q_oth, g_oth, lse_oth, kv0, kv1, kv2, kv3, *rest
):
    (
        dq_own, dq_oth, out0, out1, out2, out3,
        pos_s, key_s, val_s, rows_q, rows_g, prob_s, gp_s, half_s, ds_s,
    ) = rest[-15:]
    step = pl.program_id(0)
    core, a0, first = (meta[i] for i in range(3))
    pieces = (kv0, kv1, kv2, kv3)
    outs = (out0, out1, out2, out3)

    @pl.when(step == 0)
    def _():
        a_step = jnp.where(core == 0, 1, 4)
        b_step = jnp.where(core == 0, 4, 1)
        row = lax.broadcasted_iota(jnp.int32, (BLOCK, 128), 0)
        base = (((row >> 4) & 3) * 16 + (row >> 6) * b_step) * 256 + (row & 15)
        for a, piece in enumerate(pieces):
            slab = (a0 ^ APART[a]) * a_step
            sl = slice(a * BLOCK, (a + 1) * BLOCK)
            offset = piece[BLOCK:, :128].astype(jnp.float32).reshape(SLAB, 1, 128)
            offset = jnp.broadcast_to(offset, (SLAB, SLAB, 128)).reshape(BLOCK, 128)
            pos_s[sl, :] = offset + (base + slab * 256).astype(jnp.float32)
            for h in range(PAIR):
                key_s[h, sl, :] = piece[:BLOCK, h * 128:(h + 1) * 128]
                val_s[h, sl, :] = piece[:BLOCK, COLS + h * 128:COLS + (h + 1) * 128]

    lane = lax.broadcasted_iota(jnp.int32, (1, 128), 1)
    q_pos = [(first + lane + c * 128).astype(jnp.float32) for c in range(2)]
    sides = ((q_own, g_own, lse_own, dq_own), (q_oth, g_oth, lse_oth, dq_oth))

    for layer, (q_ref, g_ref, _, _) in enumerate(sides):
        for h in range(GROUP):
            rows = slice(layer * WIDE + h * ROWS, layer * WIDE + (h + 1) * ROWS)
            rows_q[rows, :] = q_ref[:, h * 128:(h + 1) * 128]
            rows_g[rows, :] = g_ref[:, h * 128:(h + 1) * 128]

    for layer, (_, _, lse_ref, _) in enumerate(sides):
        rows = slice(layer * WIDE, (layer + 1) * WIDE)
        lse = lse_ref[0] * LOG2E
        delta = jnp.zeros((1, WIDE), jnp.float32)
        for low in range(0, KEYS, BLOCK):
            sl = slice(low, low + BLOCK)
            score = matmul(key_s[step, sl, :], rows_q[rows, :], (1, 1))
            prob = jnp.exp2(score * (SCALE * LOG2E) - lse)
            seen = jnp.concatenate([pos_s[sl, :] <= q_pos[0], pos_s[sl, :] <= q_pos[1]] * GROUP, axis=1)
            prob = jnp.where(seen, prob, 0.0)
            grad_prob = matmul(val_s[step, sl, :], rows_g[rows, :], (1, 1))
            delta = delta + jnp.sum(prob * grad_prob, axis=0, keepdims=True)
            prob_s[layer, sl, :] = prob
            gp_s[layer, sl, :] = grad_prob
            half_s[sl, rows] = prob.astype(jnp.bfloat16)
        for low in range(0, KEYS, BLOCK):
            sl = slice(low, low + BLOCK)
            ds_s[sl, rows] = (prob_s[layer, sl, :] * (gp_s[layer, sl, :] - delta)).astype(jnp.bfloat16)

    dv = matmul(half_s[...], rows_g[...], (1, 0))
    dk = matmul(ds_s[...], rows_q[...], (1, 0)) * SCALE
    for a, out in enumerate(outs):
        sl = slice(a * BLOCK, (a + 1) * BLOCK)
        out[:, :, 0] = dk[sl].astype(out.dtype).reshape(4, 4, SLAB, HEAD_DIM)
        out[:, :, 1] = dv[sl].astype(out.dtype).reshape(4, 4, SLAB, HEAD_DIM)

    for layer, (_, _, _, dq_ref) in enumerate(sides):
        rows = slice(layer * WIDE, (layer + 1) * WIDE)
        dq_t = matmul(key_s[step], ds_s[:, rows], (0, 0)) * SCALE
        for h in range(GROUP):
            dq_ref[:, h * 128:(h + 1) * 128] = dq_t[:, h * ROWS:(h + 1) * ROWS].T


def attention(chunk, meta, q_own, g_own, lse_own, q_oth, g_oth, lse_oth, kv, partly):
    def head(g, m):
        return chunk * 4 + m[0] * 2 + g

    q_own, g_own = (pltpu.with_memory_space_constraint(v, pltpu.HBM) for v in (q_own, g_own))
    f32, bf16 = jnp.float32, jnp.bfloat16
    width = GROUP * HEAD_DIM
    own = pl.BlockSpec((ROWS, width), lambda g, m: (0, head(g, m)))
    back = pl.BlockSpec((ROWS, width), lambda g, m: (0, chunk * 2 + g))
    part = pl.BlockSpec(kv[0].shape, lambda g, m: (0, 0))
    lse = pl.BlockSpec((1, 1, WIDE), lambda g, m: (head(g, m), 0, 0))
    out_dims = (4, 4, 2, SLAB, PAIR * HEAD_DIM)
    out = pl.BlockSpec((4, 4, 2, SLAB, HEAD_DIM), lambda g, m: (0, 0, 0, 0, g))
    return pl.pallas_call(
        attention_kernel,
        grid_spec=pltpu.PrefetchScalarGridSpec(
            num_scalar_prefetch=1,
            grid=(PAIR,),
            in_specs=[own, own, lse, own, own, lse, part, part, part, part]
            + [pl.BlockSpec(memory_space=pl.ANY)] * len(partly),
            out_specs=[own, back, out, out, out, out],
            scratch_shapes=[
                pltpu.VMEM((KEYS, 128), f32),
                pltpu.VMEM((PAIR, KEYS, HEAD_DIM), bf16),
                pltpu.VMEM((PAIR, KEYS, HEAD_DIM), bf16),
                pltpu.VMEM((2 * WIDE, HEAD_DIM), bf16),
                pltpu.VMEM((2 * WIDE, HEAD_DIM), bf16),
                pltpu.VMEM((2, KEYS, WIDE), f32),
                pltpu.VMEM((2, KEYS, WIDE), f32),
                pltpu.VMEM((KEYS, 2 * WIDE), bf16),
                pltpu.VMEM((KEYS, 2 * WIDE), bf16),
            ],
        ),
        out_shape=[
            pltpu.HBM((ROWS, KV_HEADS * width), f32),
            pltpu.HBM((ROWS, KV_HEADS // 2 * width), f32),
            pltpu.HBM(out_dims, f32),
        ] + [pltpu.HBM(out_dims, bf16)] * 3,
        input_output_aliases={11 + n: n for n in range(len(partly))},
        compiler_params=pltpu.CompilerParams(vmem_limit_bytes=36 * 2**20),
        cost_estimate=pl.CostEstimate(
            flops=8 * 10**9, bytes_accessed=8 * 2**20, transcendentals=3 * 10**6
        ),
        name="attention_backward",
    )(meta, q_own, g_own, lse_own, q_oth, g_oth, lse_oth, *kv, *partly)


VMEM = pl.BlockSpec(memory_space=pltpu.VMEM)


def pack_kernel(starts, keys, values, out):
    core, zh, x, y = (lax.axis_index(n) for n in ("core", "zh", "x", "y"))
    offset = starts[0] - (zh * 16 + x * 4 + y) * 256
    tail = jnp.full((SLAB, 128), offset, jnp.int32).astype(jnp.float32).astype(jnp.bfloat16)
    for chunk in range(2):
        cols = pl.ds(pl.multiple_of(chunk * 512 + core * COLS, 128), COLS)
        out[chunk, :, :COLS] = keys[:, cols]
        out[chunk, :, COLS:2 * COLS] = values[:, cols]
        out[chunk, :, 2 * COLS:] = tail


def pack(starts, keys, values):
    keys, values = (pltpu.with_memory_space_constraint(v, pltpu.HBM) for v in (keys, values))
    return pl.pallas_call(
        pack_kernel,
        in_specs=[pl.BlockSpec(memory_space=pltpu.SMEM), VMEM, VMEM],
        out_specs=VMEM,
        out_shape=jax.ShapeDtypeStruct((2, SLAB, PAYLOAD), jnp.bfloat16),
        compiler_params=SMALL,
        name="pack_keys_values",
    )(starts, keys, values)


def line_kernel(own, far, near, next_, out):
    zl, zh = lax.axis_index("zl"), lax.axis_index("zh")
    step = jnp.where(zl == 0, -1, 1)
    for by, block in ((0, own), (2, far), (step, near), (-step, next_)):
        out[:, (zh + by) & 3] = block[...]


def line(blocks):
    return pl.pallas_call(
        line_kernel,
        in_specs=[VMEM] * 4,
        out_specs=VMEM,
        out_shape=jax.ShapeDtypeStruct((2, 4, SLAB, PAYLOAD), jnp.bfloat16),
        compiler_params=SMALL,
        name="join_line",
    )(*blocks)


def plane_place():
    core, x, y = (lax.axis_index(n) for n in ("core", "x", "y"))
    return jnp.where(core == 0, x, y)


def pieces_kernel(*refs):
    b0 = plane_place()
    row = lax.broadcasted_iota(jnp.int32, (SLAB, 128), 0)
    for chunk, out in enumerate(refs[4:]):
        tail = jnp.zeros((SLAB, 128), jnp.float32)
        for r, block in enumerate(refs[:4]):
            for z in range(4):
                place = (b0 ^ APART[r]) * 4 + z
                out[place] = block[chunk, z, :, :2 * COLS]
                offset = block[chunk, z, :, 2 * COLS:].astype(jnp.float32)
                tail = jnp.where(row == place, offset, tail)
        out[SLAB] = jnp.concatenate([tail] * (2 * COLS // 128), 1).astype(jnp.bfloat16)


def pieces_of(blocks):
    shape = jax.ShapeDtypeStruct((SLAB + 1, SLAB, 2 * COLS), jnp.bfloat16)
    return pl.pallas_call(
        pieces_kernel,
        in_specs=[VMEM] * 4,
        out_specs=[VMEM, VMEM],
        out_shape=[shape, shape],
        compiler_params=SMALL,
        name="join_pieces",
    )(*blocks)


def share_kernel(*refs):
    b0 = plane_place()
    for r, out in enumerate(refs[-4:]):
        total = refs[0][b0 ^ APART[r]]
        for ref in refs[1:4]:
            total = total + ref[b0 ^ APART[r]].astype(jnp.float32)
        out[0] = total.astype(out.dtype)


def share(chunk, terms, partly):
    dims = terms[0].shape
    whole = pl.BlockSpec(dims, lambda i: (0,) * 5)
    out_dims = (2, *dims[1:])
    return pl.pallas_call(
        share_kernel,
        grid=(1,),
        in_specs=[whole] * 4 + [pl.BlockSpec(memory_space=pl.ANY)] * len(partly),
        out_specs=[pl.BlockSpec((1, *dims[1:]), lambda i: (chunk, 0, 0, 0, 0))] * 4,
        out_shape=[jax.ShapeDtypeStruct(out_dims, jnp.float32)]
        + [jax.ShapeDtypeStruct(out_dims, jnp.bfloat16)] * 3,
        input_output_aliases={4 + n: n for n in range(len(partly))},
        compiler_params=SMALL,
        name="add_first",
    )(*terms, *partly)


def finish_kernel(got, dk, dv):
    for n, out in enumerate((dk, dv)):
        total = got[0, n].astype(jnp.float32)
        for i in range(1, 8):
            total = total + got[i, n].astype(jnp.float32)
        out[...] = total


def finish(got):
    shape = jax.ShapeDtypeStruct((SLAB, 2 * HEAD_DIM), jnp.float32)
    return pl.pallas_call(finish_kernel, out_shape=[shape, shape], compiler_params=SMALL, name="add_last")(got)


def plane_swap(value, by, x_core):
    pairs = []
    for core in range(2):
        for x in range(4):
            for y in range(4):
                to = (x ^ by, y) if core == x_core else (x, y ^ by)
                pairs.append((core * 16 + x * 4 + y, core * 16 + to[0] * 4 + to[1]))
    return lax.ppermute(value, ("core", "x", "y"), pairs)


def plane_swaps(values, x_core):
    return [plane_swap(value, by, x_core) for value, by in zip(values, APART[1:])]


def z_shift(value, by):
    pairs = []
    for z in range(8):
        up = z % 2 == 1
        to = (z + (by if up else -by)) % 8
        pairs.append((z % 2 * 4 + z // 2, to % 2 * 4 + to // 2))
    return lax.ppermute(value, ("zl", "zh"), pairs)


def add(terms):
    total = terms[0].astype(jnp.float32)
    for term in terms[1:]:
        total = total + term.astype(jnp.float32)
    return total.astype(jnp.bfloat16)


def swap(value):
    return lax.ppermute(value, "core", [(0, 1), (1, 0)])


def per_device(
    queries, out_grads, logsumexp, shared_keys, shared_values, query_starts, slab_starts
):
    core, x, y = (lax.axis_index(n) for n in ("core", "x", "y"))
    other = 1 - core
    queries, out_grads, lse = queries[0], out_grads[0], logsumexp[0]

    with jax.named_scope("gather_keys"):
        payload = pack(slab_starts, shared_keys, shared_values)
        q_sent, g_sent, payload = lax.optimization_barrier((queries, out_grads, payload))
        block = line([payload] + [z_shift(payload, by) for by in (3, 1, 2)])
        with jax.named_scope("swap_queries"):
            q_oth, g_oth, lse_oth = (swap(v) for v in (q_sent, g_sent, lse))
        blocks = [block] + plane_swaps([block] * 3, 0)
        wide = (KV_HEADS, 1, WIDE)
        blocks, q_oth, g_oth, lse, lse_oth = lax.optimization_barrier(
            (blocks, q_oth, g_oth, lse.reshape(wide), lse_oth.reshape(wide))
        )
        own = pieces_of(blocks)
        pieces = []
        for piece in own:
            piece = piece.reshape(BLOCK + SLAB, 2 * COLS)
            pieces.append([piece] + plane_swaps([piece] * 3, 1))
    a0 = jnp.where(core == 0, y, x)
    meta = jnp.stack([core, a0, query_starts[0]]).astype(jnp.int32)
    partly, sums = [], []
    for chunk in range(2):
        *partly, part0, part1, part2, part3 = attention(
            chunk, meta, queries, out_grads, lse, q_oth, g_oth, lse_oth, pieces[chunk], partly
        )
        with jax.named_scope("scatter_grads"):
            if sums:
                part0, part1, part2, part3, partly, sums = lax.optimization_barrier(
                    (part0, part1, part2, part3, partly, sums)
                )
            sums.append([part0, *plane_swaps([part1, part2, part3], 1)])

    dq, dq_oth = partly
    with jax.named_scope("scatter_grads"):
        first_shares = share(0, sums[0], [])
    with jax.named_scope("swap_query_grads"):
        dq_oth, first_shares = lax.optimization_barrier((dq_oth, first_shares))
        back = swap(dq_oth)
        dq = lax.dynamic_update_slice(dq, back[:, :768], (0, other * 768))
        dq = lax.dynamic_update_slice(dq, back[:, 768:], (0, (2 + other) * 768))
    with jax.named_scope("scatter_grads"):
        mine, *shares = share(1, sums[1], first_shares)
        shares = plane_swaps(shares, 0)
        shares[0], dq = lax.optimization_barrier((shares[0], dq))
        small = add([mine, *shares]).reshape(8, 2, SLAB, 2 * HEAD_DIM)
        dk, dv = finish(lax.all_to_all(small, ("zl", "zh"), 0, 0))
    return dq[None], dk, dv


def solution(mesh):
    fine = Mesh(mesh.devices.reshape(2, 2, 4, 4, 4), AXES)
    section, seq = ("zl", "core"), ("zh", "x", "y")
    return jax.shard_map(
        per_device,
        mesh=fine,
        in_specs=(
            P(section, seq, None),
            P(section, seq, None),
            P(section, None, seq),
            P(seq, None),
            P(seq, None),
            P(seq),
            P(seq),
        ),
        out_specs=(P(section, seq, None), P(seq, section), P(seq, section)),
        check_vma=False,
    )
```
